256 devices in a mesh: seq: 64 (over y, x, z_hi, core), chan: 4 (over z_lo).
Axes of the slice: x: 4, y: 4, z: 8 (z_hi: 2, z_lo: 4; z = z_hi * 4 + z_lo), core: 2. Of those that a mesh axis runs over, the one named last changes fastest.
Arguments:
- signal: float32 [1024, 32768], P('chan', 'seq'), may hold values from -6 to 6
- gate: float32 [1024, 32768], P('chan', 'seq'), may hold values from -6 to 6
- filter_taps: float32 [1024, 32768], P('chan', 'seq'), may hold values from -2.5 to 2.5
- skip_weight: float32 [1024], P('chan'), may hold values from -1 to 1
- out_weight: bfloat16 [1024, 8192], P('chan'), may hold values from -0.1875 to 0.1875
Outputs:
- mixed: float32 [1024, 32768], P('chan', 'seq')
- projected: bfloat16 [32768, 8192], P(('seq', 'chan'))
The draws below stay inside these ranges and needn't reach their ends.
All inputs are finite; a program needn't handle non-finite values.
Results may differ from the reference program's by a relative error of at most 0.023.
Values may be sent and summed in bfloat16 or wider, within the bound.
No kernel may reach another device: no remote copies, remote signals or barrier semaphores. Data moves between devices by JAX's collectives and lax.ppermute only.
A program may use at most 128 MiB of HBM per device.

```python
import math
import jax
import jax.numpy as jnp
from jax import lax

WIDTH = 8192
SLAB_CHANNELS = 1024
TOTAL_POSITIONS = 32768
N_CHAN = 4


def draw_filter_taps(key, part):
    random_subkeys = jax.random.split(key, 6)
    positions = jnp.arange(TOTAL_POSITIONS, dtype=jnp.float32)[None, :]
    position_numbers = jnp.arange(TOTAL_POSITIONS, dtype=jnp.int32)[None, :]
    slow_mask = jax.random.bernoulli(random_subkeys[0], 0.5, (SLAB_CHANNELS, 1))
    rough_part = jax.random.truncated_normal(random_subkeys[1], -4.0, 4.0, (SLAB_CHANNELS, TOTAL_POSITIONS), jnp.float32)
    slow_rate = jnp.exp(jax.random.uniform(random_subkeys[2], (SLAB_CHANNELS, 1), jnp.float32, math.log(0.05), math.log(0.9))) / TOTAL_POSITIONS
    fast_rate = jnp.exp(jax.random.uniform(random_subkeys[3], (SLAB_CHANNELS, 1), jnp.float32, math.log(1.0 / 16.0), math.log(1.0 / 6.0)))
    decay_rate = jnp.where(slow_mask, slow_rate, fast_rate)
    spike_location = jax.random.randint(random_subkeys[4], (3,), 0, TOTAL_POSITIONS)
    spike_retain_mask = jax.random.uniform(random_subkeys[5], (SLAB_CHANNELS, 3), jnp.float32, 0.5, 0.8)
    decay_profile = jnp.exp(-decay_rate * positions)
    for spike_index in range(3):
        decay_profile = decay_profile * jnp.where(position_numbers >= spike_location[spike_index], spike_retain_mask[:, spike_index:spike_index + 1], 1.0)
    amplitude = jax.lax.rsqrt(jnp.minimum(jnp.float32(TOTAL_POSITIONS), 0.5 / decay_rate))
    return (amplitude * decay_profile * rough_part).astype(jnp.float32)


def levels(key, shape, cuts, low, top_value):
    loudness = 1.0
    for dim, shards_of in cuts:
        draws = jax.random.uniform(jax.random.fold_in(jax.random.fold_in(key, 6), dim), (shards_of,), jnp.float32, low / len(cuts), top_value / len(cuts))
        loudness = loudness * jnp.repeat(jnp.exp(draws), shape[dim] // shards_of).reshape((-1,) + (1,) * (len(shape) - 1 - dim))
    return loudness


def gaussian(stream_key, shape, scale, most, pieces=(), kind=jnp.bfloat16):
    result = jax.random.normal(stream_key, shape, jnp.float32) * scale
    if len(pieces) > 0:
        result = levels(stream_key, shape, pieces, -0.22, 0.18) * result
    return jnp.clip(result, min=-most, max=most).astype(kind)


def setup_inputs(seed: int = 0) -> dict:
    key_of = jax.random.split(jax.random.key(seed), 6)
    signal = gaussian(key_of[0], (SLAB_CHANNELS, TOTAL_POSITIONS), 1.0, 6.0, ((0, 4), (1, 64)), jnp.float32)
    gate = gaussian(key_of[1], (SLAB_CHANNELS, TOTAL_POSITIONS), 1.0, 6.0, ((0, 4), (1, 64)), jnp.float32)
    filter_taps = draw_filter_taps(jax.random.fold_in(key_of[5], 71), 0)
    skip_weight = jnp.clip(jax.random.uniform(key_of[3], (SLAB_CHANNELS,), jnp.float32, -1.0, 1.0) * levels(key_of[3], (SLAB_CHANNELS,), ((0, 4),), -0.4, 0.0), -1.0, 1.0)
    out_weight = gaussian(key_of[4], (SLAB_CHANNELS, WIDTH), SLAB_CHANNELS ** -0.5, 0.1875, ((0, 4),))
    return {"signal": signal, "gate": gate, "filter_taps": filter_taps, "skip_weight": skip_weight, "out_weight": out_weight}


def reference(signal, gate, filter_taps, skip_weight, out_weight):
    padded_len = 2 * TOTAL_POSITIONS
    signal_freq = jnp.fft.rfft(signal, n=padded_len, axis=1)
    filter_freq = jnp.fft.rfft(filter_taps, n=padded_len, axis=1)
    convolved = jnp.fft.irfft(signal_freq * filter_freq, n=padded_len, axis=1)[:, :TOTAL_POSITIONS]
    convolved = convolved.astype(jnp.float32)
    mixed = gate * (convolved + skip_weight[:, None] * signal)
    rounded = mixed.astype(jnp.bfloat16)
    group_size = SLAB_CHANNELS // N_CHAN
    block_rows = min(TOTAL_POSITIONS, 2048)
    column_blocks = rounded.reshape(SLAB_CHANNELS, TOTAL_POSITIONS // block_rows, block_rows).transpose(1, 0, 2)

    def project_block(columns):
        summed = jnp.zeros((block_rows, WIDTH), jnp.float32)
        for group_index in range(N_CHAN):
            part_cols = columns[group_index * group_size:(group_index + 1) * group_size]
            part_rows = out_weight[group_index * group_size:(group_index + 1) * group_size]
            partial_value = jnp.dot(part_cols.T, part_rows, preferred_element_type=jnp.float32)
            partial_value = lax.optimization_barrier(partial_value.astype(jnp.bfloat16))
            summed = summed + partial_value.astype(jnp.float32)
        return summed.astype(jnp.bfloat16)

    projected = lax.map(project_block, column_blocks).reshape(TOTAL_POSITIONS, WIDTH)
    return mixed, projected
```

```python
import functools

import jax
import jax.numpy as jnp
import ml_dtypes
import numpy as np
from jax import lax
from jax.experimental import pallas as pl
from jax.experimental.pallas import tpu as pltpu
from jax.sharding import Mesh
from jax.sharding import PartitionSpec as P

AXES = ("y", "x", "zh", "core")
SEQ_DEVICES = 64
ROWS = 256
LANES = 128
POSITIONS = ROWS * LANES
OWN_CHANNELS = 4
PIECES = 4


def transform_tables():
    n1 = (np.arange(SEQ_DEVICES)[None, :] * PIECES + np.arange(PIECES)[:, None]).reshape(-1)
    k1 = np.arange(ROWS) + 0.25
    first = np.exp(-2j * np.pi * np.outer(k1, n1) / ROWS)
    n2 = np.arange(LANES)
    turn = np.exp(-2j * np.pi * np.outer(k1, n2) / POSITIONS)
    second = np.exp(-2j * np.pi * np.outer(n2, n2) / LANES)
    forward_one = np.concatenate([first.real, first.imag], 0)
    forward_two = np.block([[second.real, second.imag], [-second.imag, second.real]])
    back_two = np.block([[second.real, -second.imag], [second.imag, second.real]])
    back_one = np.concatenate([first.real.T, first.imag.T], 1)

    def narrow(table):
        return table.astype(np.float32).astype(ml_dtypes.bfloat16)

    return (
        narrow(forward_one),
        narrow(forward_two),
        narrow(back_two),
        narrow(back_one),
        turn.real.astype(np.float32),
        turn.imag.astype(np.float32),
    )


def pack_kernel(signal_ref, filter_ref, out_ref, wide):
    for which, source in enumerate((signal_ref, filter_ref)):
        for own in range(OWN_CHANNELS):
            for piece in range(PIECES):
                row = which * 16 + own * PIECES + piece
                wide[pl.ds(row, SEQ_DEVICES, stride=32), :] = source[
                    own * SEQ_DEVICES : (own + 1) * SEQ_DEVICES,
                    piece * LANES : (piece + 1) * LANES,
                ]
    out_ref[...] = wide[...].astype(jnp.bfloat16)


def matmul(left, right):
    return jnp.dot(left, right, preferred_element_type=jnp.float32)


def convolve_kernel(
    data_ref, one_ref, two_ref, back_two_ref, back_one_ref, cos_ref, sin_ref, out_ref, wide, result
):
    wide[...] = data_ref[...].astype(jnp.float32)
    columns = []
    for which in range(2):
        for own in range(OWN_CHANNELS):
            pieces = [
                wide[pl.ds(which * 16 + own * PIECES + piece, SEQ_DEVICES, stride=32), :]
                for piece in range(PIECES)
            ]
            columns.append(jnp.concatenate(pieces, axis=0).astype(jnp.bfloat16))
    turn_cos, turn_sin = cos_ref[...], sin_ref[...]

    def spectrum(column):
        part = matmul(one_ref[...], column)
        real, imag = part[:ROWS], part[ROWS:]
        turned = jnp.concatenate(
            [real * turn_cos - imag * turn_sin, real * turn_sin + imag * turn_cos], axis=1
        )
        both = matmul(turned.astype(jnp.bfloat16), two_ref[...])
        return both[:, :LANES], both[:, LANES:]

    for own in range(OWN_CHANNELS):
        signal_real, signal_imag = spectrum(columns[own])
        filter_real, filter_imag = spectrum(columns[OWN_CHANNELS + own])
        product = jnp.concatenate(
            [
                signal_real * filter_real - signal_imag * filter_imag,
                signal_real * filter_imag + signal_imag * filter_real,
            ],
            axis=1,
        )
        back = matmul(product.astype(jnp.bfloat16), back_two_ref[...])
        real, imag = back[:, :LANES], back[:, LANES:]
        turned = jnp.concatenate(
            [real * turn_cos + imag * turn_sin, imag * turn_cos - real * turn_sin], axis=0
        )
        values = matmul(back_one_ref[...], turned.astype(jnp.bfloat16)) * (1.0 / POSITIONS)
        for piece in range(PIECES):
            result[pl.ds(own * PIECES + piece, SEQ_DEVICES, stride=16), :] = values[
                piece * SEQ_DEVICES : (piece + 1) * SEQ_DEVICES
            ]
    out_ref[...] = result[...].astype(jnp.bfloat16)


def mix_kernel(conv_ref, signal_ref, gate_ref, skip_ref, mixed_ref, rounded_ref, wide):
    wide[...] = conv_ref[...].astype(jnp.float32)
    for own in range(OWN_CHANNELS):
        rows = slice(own * SEQ_DEVICES, (own + 1) * SEQ_DEVICES)
        skip = skip_ref[rows, :]
        for piece in range(PIECES):
            lanes = slice(piece * LANES, (piece + 1) * LANES)
            conv = wide[pl.ds(own * PIECES + piece, SEQ_DEVICES, stride=16), :]
            mixed = gate_ref[rows, lanes] * (conv + skip * signal_ref[rows, lanes])
            mixed_ref[rows, lanes] = mixed
            rounded_ref[piece, rows, :] = mixed.astype(jnp.bfloat16)


def call(kernel, out_shape, scratch, cost=None):
    return pl.pallas_call(
        kernel, out_shape=out_shape, scratch_shapes=scratch, cost_estimate=cost
    )


def gathered_weights(out_weight):
    half = out_weight.shape[1] // 2
    piece = half // 16
    place = lax.axis_index("y") * 4 + lax.axis_index("x")
    start = lax.axis_index("core") * half + place * piece
    mine = lax.dynamic_slice_in_dim(out_weight, start, piece, 1)
    depth = lax.all_gather(mine, "chan", axis=0, tiled=True)
    return lax.all_gather(depth, ("y", "x"), axis=0, tiled=False)


def body(signal, gate, filter_taps, skip_weight, out_weight):
    weights = gathered_weights(out_weight)
    tables = transform_tables()
    packed = call(
        pack_kernel,
        jax.ShapeDtypeStruct((SEQ_DEVICES * 32, LANES), jnp.bfloat16),
        [pltpu.VMEM((SEQ_DEVICES * 32, LANES), jnp.float32)],
    )(signal, filter_taps)
    arrived = lax.all_to_all(
        packed.reshape(SEQ_DEVICES, 32, LANES), AXES, split_axis=0, concat_axis=0, tiled=True
    )
    convolved = call(
        convolve_kernel,
        jax.ShapeDtypeStruct((SEQ_DEVICES * 16, LANES), jnp.bfloat16),
        [
            pltpu.VMEM((SEQ_DEVICES * 32, LANES), jnp.float32),
            pltpu.VMEM((SEQ_DEVICES * 16, LANES), jnp.float32),
        ],
    )(arrived.reshape(SEQ_DEVICES * 32, LANES), *tables)
    returned = lax.all_to_all(
        convolved.reshape(SEQ_DEVICES, 16, LANES), AXES, split_axis=0, concat_axis=0, tiled=True
    )
    channels, shard_len = signal.shape
    mixed, rounded = call(
        mix_kernel,
        (
            jax.ShapeDtypeStruct((channels, shard_len), jnp.float32),
            jax.ShapeDtypeStruct((PIECES, channels, LANES), jnp.bfloat16),
        ),
        [pltpu.VMEM((SEQ_DEVICES * 16, LANES), jnp.float32)],
    )(returned.reshape(SEQ_DEVICES * 16, LANES), signal, gate, skip_weight[:, None])
    mine = lax.all_to_all(rounded, "chan", split_axis=0, concat_axis=0, tiled=True)
    mine = mine.reshape(4 * channels, LANES)
    pair = [(0, 1), (1, 0)]
    theirs = lax.ppermute(mine, "core", pair)

    def project(columns):
        return (
            jnp.einsum("ct,gcm->tgm", columns, weights, preferred_element_type=jnp.float32)
            .astype(jnp.bfloat16)
            .reshape(LANES, -1)
        )

    for_them = project(theirs)
    from_them = lax.ppermute(for_them, "core", pair)
    own = project(mine)
    first_core = lax.axis_index("core") == 0
    projected = jnp.concatenate(
        [jnp.where(first_core, own, from_them), jnp.where(first_core, from_them, own)], axis=1
    )
    return mixed, projected


def solution(mesh):
    fine = Mesh(mesh.devices.reshape(4, 4, 2, 2, 4), (*AXES, "chan"))
    slab = P("chan", AXES)
    in_specs = (slab, slab, slab, P("chan"), P("chan", None))
    out_specs = (slab, P((*AXES, "chan"), None))
    return jax.shard_map(body, mesh=fine, in_specs=in_specs, out_specs=out_specs, check_vma=False)
```

```python
import itertools

import jax
import jax.numpy as jnp
import ml_dtypes
import numpy as np
from jax import lax
from jax.experimental import pallas as pl
from jax.experimental.pallas import tpu as pltpu
from jax.sharding import Mesh
from jax.sharding import PartitionSpec as P

AXES = ("y", "x", "zh", "core")
SEQ_DEVICES = 64
ROWS = 256
LANES = 128
POSITIONS = ROWS * LANES
OWN_CHANNELS = 4
PIECES = 4
HALF = 4096
QUARTER = 1024
WORK = 10**11


def transform_tables():
    n1 = (np.arange(SEQ_DEVICES)[None, :] * PIECES + np.arange(PIECES)[:, None]).reshape(-1)
    k1 = np.arange(ROWS) + 0.25
    first = np.exp(-2j * np.pi * np.outer(k1, n1) / ROWS)
    n2 = np.arange(LANES)
    turn = np.exp(-2j * np.pi * np.outer(k1, n2) / POSITIONS)
    second = np.exp(-2j * np.pi * np.outer(n2, n2) / LANES)
    forward_one = np.concatenate([first.real, first.imag], 0)
    forward_two = np.block([[second.real, second.imag], [-second.imag, second.real]])
    back_two = np.block([[second.real, -second.imag], [second.imag, second.real]])
    back_one = np.concatenate([first.real.T, first.imag.T], 1)

    def narrow(table):
        return table.astype(np.float32).astype(ml_dtypes.bfloat16)

    return (
        narrow(forward_one),
        narrow(forward_two),
        narrow(back_two),
        narrow(back_one),
        turn.real.astype(np.float32),
        turn.imag.astype(np.float32),
    )


def pack_kernel(signal_ref, filter_ref, out_ref, wide):
    for which, source in enumerate((signal_ref, filter_ref)):
        for own in range(OWN_CHANNELS):
            for piece in range(PIECES):
                row = which * 16 + own * PIECES + piece
                wide[pl.ds(row, SEQ_DEVICES, stride=32), :] = source[
                    own * SEQ_DEVICES : (own + 1) * SEQ_DEVICES,
                    piece * LANES : (piece + 1) * LANES,
                ]
    out_ref[...] = wide[...].astype(jnp.bfloat16)


def matmul(left, right):
    return jnp.dot(left, right, preferred_element_type=jnp.float32)


def convolve_kernel(
    data_ref, one_ref, two_ref, back_two_ref, back_one_ref, cos_ref, sin_ref, out_ref, wide, result
):
    wide[...] = data_ref[...].astype(jnp.float32)
    columns = []
    for which in range(2):
        for own in range(OWN_CHANNELS):
            pieces = [
                wide[pl.ds(which * 16 + own * PIECES + piece, SEQ_DEVICES, stride=32), :]
                for piece in range(PIECES)
            ]
            columns.append(jnp.concatenate(pieces, axis=0).astype(jnp.bfloat16))
    turn_cos, turn_sin = cos_ref[...], sin_ref[...]

    def spectrum(column):
        part = matmul(one_ref[...], column)
        real, imag = part[:ROWS], part[ROWS:]
        turned = jnp.concatenate(
            [real * turn_cos - imag * turn_sin, real * turn_sin + imag * turn_cos], axis=1
        )
        both = matmul(turned.astype(jnp.bfloat16), two_ref[...])
        return both[:, :LANES], both[:, LANES:]

    for own in range(OWN_CHANNELS):
        signal_real, signal_imag = spectrum(columns[own])
        filter_real, filter_imag = spectrum(columns[OWN_CHANNELS + own])
        product = jnp.concatenate(
            [
                signal_real * filter_real - signal_imag * filter_imag,
                signal_real * filter_imag + signal_imag * filter_real,
            ],
            axis=1,
        )
        back = matmul(product.astype(jnp.bfloat16), back_two_ref[...])
        real, imag = back[:, :LANES], back[:, LANES:]
        turned = jnp.concatenate(
            [real * turn_cos + imag * turn_sin, imag * turn_cos - real * turn_sin], axis=0
        )
        values = matmul(back_one_ref[...], turned.astype(jnp.bfloat16)) * (1.0 / POSITIONS)
        for piece in range(PIECES):
            result[pl.ds(own * PIECES + piece, SEQ_DEVICES, stride=16), :] = values[
                piece * SEQ_DEVICES : (piece + 1) * SEQ_DEVICES
            ]
    out_ref[...] = result[...].astype(jnp.bfloat16)


def mix_kernel(conv_ref, signal_ref, gate_ref, skip_ref, mixed_ref, rounded_ref, wide):
    wide[...] = conv_ref[...].astype(jnp.float32)
    for own in range(OWN_CHANNELS):
        rows = slice(own * SEQ_DEVICES, (own + 1) * SEQ_DEVICES)
        skip = skip_ref[rows, :]
        for piece in range(PIECES):
            lanes = slice(piece * LANES, (piece + 1) * LANES)
            conv = wide[pl.ds(own * PIECES + piece, SEQ_DEVICES, stride=16), :]
            mixed = gate_ref[rows, lanes] * (conv + skip * signal_ref[rows, lanes])
            mixed_ref[rows, lanes] = mixed
            rounded_ref[piece, rows, :] = mixed.astype(jnp.bfloat16)


def call(kernel, out_shape, scratch, limit=8, work=0, **options):
    return pl.pallas_call(
        kernel,
        out_shape=out_shape,
        scratch_shapes=scratch,
        compiler_params=pltpu.CompilerParams(vmem_limit_bytes=limit << 20),
        cost_estimate=pl.CostEstimate(flops=work, bytes_accessed=0, transcendentals=0),
        **options,
    )


def device_pairs(move):
    pairs = []
    for y, x, z, core in itertools.product(range(4), range(4), range(8), range(2)):
        spots = []
        for sy, sx, sz, sc in ((y, x, z, core), move(y, x, z, core)):
            sy, sx, sz = sy % 4, sx % 4, sz % 8
            spots.append((((sy * 4 + sx) * 2 + sz // 4) * 2 + sc) * 4 + sz % 4)
        pairs.append(tuple(spots))
    return pairs


def moved(array, move):
    return lax.ppermute(array, (*AXES, "chan"), device_pairs(move))


def colour():
    return (lax.axis_index("x") + 2 * lax.axis_index("y")) % 4


def join_kernel(below_ref, above_ref, far_ref, after_ref, out_ref, sem):
    copies = [
        pltpu.make_async_copy(ref, out_ref.at[pl.ds(index * ROWS, ROWS)], sem.at[index])
        for index, ref in enumerate((below_ref, above_ref, far_ref))
    ]
    for copy in copies:
        copy.start()
    for copy in copies:
        copy.wait()


def keep_kernel(block_ref, after_ref, out_ref):
    pass


ANYWHERE = pl.BlockSpec(memory_space=pl.ANY)


def ordered(block, after):
    return call(
        keep_kernel,
        jax.ShapeDtypeStruct(block.shape, block.dtype),
        [],
        limit=4,
        in_specs=[ANYWHERE] * 2,
        out_specs=ANYWHERE,
        input_output_aliases={0: 0},
    )(block, after)


def first_quarter(out_weight):
    start = lax.axis_index("core") * HALF + colour() * QUARTER
    mine = lax.dynamic_slice_in_dim(out_weight, start, QUARTER, 1)
    below = moved(mine, lambda y, x, z, c: (y, x, z + 1, c))
    above = moved(mine, lambda y, x, z, c: (y, x, z - 1, c))
    far = moved(mine, lambda y, x, z, c: (y, x, z + 2 - 4 * c, c))
    return below, above, far


def other_quarters(parts, after):
    block = call(
        join_kernel,
        jax.ShapeDtypeStruct((3 * ROWS, QUARTER), jnp.bfloat16),
        [pltpu.SemaphoreType.DMA((3,))],
        limit=4,
        in_specs=[ANYWHERE] * 4,
        out_specs=ANYWHERE,
    )(*parts, after)
    return [
        block,
        moved(block, lambda y, x, z, c: (y, x - 1, z, c)),
        moved(block, lambda y, x, z, c: (y + 1 - 2 * c, x, z, c)),
        moved(block, lambda y, x, z, c: (y, x + 1, z, c)),
    ]


def both_halves(blocks, after):
    blocks = blocks[:1] + [ordered(block, after) for block in blocks[1:]]
    return blocks + [moved(block, lambda y, x, z, c: (y, x, z, 1 - c)) for block in blocks]


def project_kernel(columns_ref, own_ref, *refs):
    block_refs, (out_ref, weights, results, own_sem, block_sem, out_sem) = refs[:8], refs[8:]
    core, chan = lax.axis_index("core"), lax.axis_index("chan")
    starts, loads = [], []
    for index, block_ref in enumerate(block_refs):
        half = core if index < 4 else 1 - core
        start = pl.multiple_of(half * HALF + (colour() + index) % 4 * QUARTER, QUARTER)
        pair = (
            pltpu.make_async_copy(
                own_ref.at[:, pl.ds(start, QUARTER)],
                weights.at[index, pl.ds(0, ROWS)],
                own_sem.at[index],
            ),
            pltpu.make_async_copy(
                block_ref, weights.at[index, pl.ds(ROWS, 3 * ROWS)], block_sem.at[index]
            ),
        )
        for load in pair:
            load.start()
        starts.append(start)
        loads.append(pair)
    rows = [
        columns_ref[pl.ds(pl.multiple_of((chan + shift) % 4 * ROWS, ROWS), ROWS), :].T
        for shift in (0, 3, 1, 2)
    ]
    left = jnp.concatenate(rows, axis=1)
    stores = []
    for index in range(8):
        for load in loads[index]:
            load.wait()
        results[index] = matmul(left, weights[index]).astype(jnp.bfloat16)
        store = pltpu.make_async_copy(
            results.at[index], out_ref.at[:, pl.ds(starts[index], QUARTER)], out_sem.at[index]
        )
        store.start()
        stores.append(store)
    for store in stores:
        store.wait()


def body(signal, gate, filter_taps, skip_weight, out_weight):
    parts = first_quarter(out_weight)
    tables = transform_tables()
    packed = call(
        pack_kernel,
        jax.ShapeDtypeStruct((SEQ_DEVICES * 32, LANES), jnp.bfloat16),
        [pltpu.VMEM((SEQ_DEVICES * 32, LANES), jnp.float32)],
        work=WORK,
    )(signal, filter_taps)
    blocks = other_quarters(parts, packed)
    arrived = lax.all_to_all(
        packed.reshape(SEQ_DEVICES, 32, LANES), AXES, split_axis=0, concat_axis=0, tiled=True
    )
    convolved = call(
        convolve_kernel,
        jax.ShapeDtypeStruct((SEQ_DEVICES * 16, LANES), jnp.bfloat16),
        [
            pltpu.VMEM((SEQ_DEVICES * 32, LANES), jnp.float32),
            pltpu.VMEM((SEQ_DEVICES * 16, LANES), jnp.float32),
        ],
        work=WORK,
    )(arrived.reshape(SEQ_DEVICES * 32, LANES), *tables)
    weights = both_halves(blocks, convolved)
    returned = lax.all_to_all(
        convolved.reshape(SEQ_DEVICES, 16, LANES), AXES, split_axis=0, concat_axis=0, tiled=True
    )
    channels, shard_len = signal.shape
    mixed, rounded = call(
        mix_kernel,
        (
            jax.ShapeDtypeStruct((channels, shard_len), jnp.float32),
            jax.ShapeDtypeStruct((PIECES, channels, LANES), jnp.bfloat16),
        ),
        [pltpu.VMEM((SEQ_DEVICES * 16, LANES), jnp.float32)],
        work=WORK,
    )(returned.reshape(SEQ_DEVICES * 16, LANES), signal, gate, skip_weight[:, None])
    mine = lax.all_to_all(rounded, "chan", split_axis=0, concat_axis=0, tiled=True)
    width = out_weight.shape[1]
    projected = call(
        project_kernel,
        jax.ShapeDtypeStruct((LANES, width), jnp.bfloat16),
        [
            pltpu.VMEM((8, 4 * ROWS, QUARTER), jnp.bfloat16),
            pltpu.VMEM((8, LANES, QUARTER), jnp.bfloat16),
            pltpu.SemaphoreType.DMA((8,)),
            pltpu.SemaphoreType.DMA((8,)),
            pltpu.SemaphoreType.DMA((8,)),
        ],
        limit=58,
        in_specs=[pl.BlockSpec(memory_space=pltpu.VMEM)] + [ANYWHERE] * 9,
        out_specs=ANYWHERE,
    )(mine.reshape(4 * channels, LANES), out_weight, *weights)
    return mixed, projected


def solution(mesh):
    fine = Mesh(mesh.devices.reshape(4, 4, 2, 2, 4), (*AXES, "chan"))
    slab = P("chan", AXES)
    in_specs = (slab, slab, slab, P("chan"), P("chan", None))
    out_specs = (slab, P((*AXES, "chan"), None))
    return jax.shard_map(body, mesh=fine, in_specs=in_specs, out_specs=out_specs, check_vma=False)
```

```python
import itertools

import jax
import jax.numpy as jnp
import ml_dtypes
import numpy as np
from jax import lax
from jax.experimental import pallas as pl
from jax.experimental.pallas import tpu as pltpu
from jax.sharding import Mesh
from jax.sharding import PartitionSpec as P

AXES = ("y", "x", "zh", "core")
SEQ_DEVICES = 64
ROWS = 256
LANES = 128
POSITIONS = ROWS * LANES
OWN_CHANNELS = 4
PIECES = 4
HALF = 4096
QUARTER = 1024
SPLIT = 384
WORK = 10**11
PACK_WORK = 10**10
JOIN_WORK = 10**10


def transform_tables():
    n1 = (np.arange(SEQ_DEVICES)[None, :] * PIECES + np.arange(PIECES)[:, None]).reshape(-1)
    k1 = np.arange(ROWS) + 0.25
    first = np.exp(-2j * np.pi * np.outer(k1, n1) / ROWS)
    n2 = np.arange(LANES)
    turn = np.exp(-2j * np.pi * np.outer(k1, n2) / POSITIONS)
    second = np.exp(-2j * np.pi * np.outer(n2, n2) / LANES)
    forward_one = np.concatenate([first.real, first.imag], 0)
    forward_two = np.block([[second.real, second.imag], [-second.imag, second.real]])
    back_two = np.block([[second.real, -second.imag], [second.imag, second.real]])
    back_one = np.concatenate([first.real.T, first.imag.T], 1)

    def narrow(table):
        return table.astype(np.float32).astype(ml_dtypes.bfloat16)

    return (
        narrow(forward_one),
        narrow(forward_two),
        narrow(back_two),
        narrow(back_one),
        turn.real.astype(np.float32),
        turn.imag.astype(np.float32),
    )


def pack_kernel(signal_ref, filter_ref, after_ref, out_ref, wide):
    for which, source in enumerate((signal_ref, filter_ref)):
        for own in range(OWN_CHANNELS):
            for piece in range(PIECES):
                row = which * 16 + own * PIECES + piece
                wide[pl.ds(row, SEQ_DEVICES, stride=32), :] = source[
                    own * SEQ_DEVICES : (own + 1) * SEQ_DEVICES,
                    piece * LANES : (piece + 1) * LANES,
                ]
    out_ref[...] = wide[...].astype(jnp.bfloat16)


def matmul(left, right):
    return jnp.dot(left, right, preferred_element_type=jnp.float32)


def convolve_kernel(
    data_ref, one_ref, two_ref, back_two_ref, back_one_ref, cos_ref, sin_ref, out_ref, wide, result
):
    wide[...] = data_ref[...].astype(jnp.float32)
    columns = []
    for which in range(2):
        for own in range(OWN_CHANNELS):
            pieces = [
                wide[pl.ds(which * 16 + own * PIECES + piece, SEQ_DEVICES, stride=32), :]
                for piece in range(PIECES)
            ]
            columns.append(jnp.concatenate(pieces, axis=0).astype(jnp.bfloat16))
    turn_cos, turn_sin = cos_ref[...], sin_ref[...]

    def spectrum(column):
        part = matmul(one_ref[...], column)
        real, imag = part[:ROWS], part[ROWS:]
        turned = jnp.concatenate(
            [real * turn_cos - imag * turn_sin, real * turn_sin + imag * turn_cos], axis=1
        )
        both = matmul(turned.astype(jnp.bfloat16), two_ref[...])
        return both[:, :LANES], both[:, LANES:]

    for own in range(OWN_CHANNELS):
        signal_real, signal_imag = spectrum(columns[own])
        filter_real, filter_imag = spectrum(columns[OWN_CHANNELS + own])
        product = jnp.concatenate(
            [
                signal_real * filter_real - signal_imag * filter_imag,
                signal_real * filter_imag + signal_imag * filter_real,
            ],
            axis=1,
        )
        back = matmul(product.astype(jnp.bfloat16), back_two_ref[...])
        real, imag = back[:, :LANES], back[:, LANES:]
        turned = jnp.concatenate(
            [real * turn_cos + imag * turn_sin, imag * turn_cos - real * turn_sin], axis=0
        )
        values = matmul(back_one_ref[...], turned.astype(jnp.bfloat16)) * (1.0 / POSITIONS)
        for piece in range(PIECES):
            result[pl.ds(own * PIECES + piece, SEQ_DEVICES, stride=16), :] = values[
                piece * SEQ_DEVICES : (piece + 1) * SEQ_DEVICES
            ]
    out_ref[...] = result[...].astype(jnp.bfloat16)


def mix_kernel(conv_ref, signal_ref, gate_ref, skip_ref, mixed_ref, rounded_ref, wide):
    wide[...] = conv_ref[...].astype(jnp.float32)
    for own in range(OWN_CHANNELS):
        rows = slice(own * SEQ_DEVICES, (own + 1) * SEQ_DEVICES)
        skip = skip_ref[rows, :]
        for piece in range(PIECES):
            lanes = slice(piece * LANES, (piece + 1) * LANES)
            conv = wide[pl.ds(own * PIECES + piece, SEQ_DEVICES, stride=16), :]
            mixed = gate_ref[rows, lanes] * (conv + skip * signal_ref[rows, lanes])
            mixed_ref[rows, lanes] = mixed
            rounded_ref[piece, rows, :] = mixed.astype(jnp.bfloat16)


def call(kernel, out_shape, scratch, limit=60, work=0, **options):
    return pl.pallas_call(
        kernel,
        out_shape=out_shape,
        scratch_shapes=scratch,
        compiler_params=pltpu.CompilerParams(vmem_limit_bytes=limit << 20),
        cost_estimate=pl.CostEstimate(flops=work, bytes_accessed=0, transcendentals=0),
        **options,
    )


def device_pairs(move):
    pairs = []
    for y, x, z, core in itertools.product(range(4), range(4), range(8), range(2)):
        spots = []
        for sy, sx, sz, sc in ((y, x, z, core), move(y, x, z, core)):
            sy, sx, sz = sy % 4, sx % 4, sz % 8
            spots.append((((sy * 4 + sx) * 2 + sz // 4) * 2 + sc) * 4 + sz % 4)
        pairs.append(tuple(spots))
    return pairs


def moved(array, move):
    return lax.ppermute(array, (*AXES, "chan"), device_pairs(move))


def colour(core):
    x, y = lax.axis_index("x"), lax.axis_index("y")
    return jnp.where(core == 0, x + 2 * y, 2 * x + y) % 4


def join_kernel(below_ref, above_ref, far_ref, after_ref, out_ref, sem):
    copies = [
        pltpu.make_async_copy(ref, out_ref.at[pl.ds(index * ROWS, ROWS)], sem.at[index])
        for index, ref in enumerate((below_ref, above_ref, far_ref))
    ]
    for copy in copies:
        copy.start()
    for copy in copies:
        copy.wait()


def keep_kernel(block_ref, after_ref, out_ref):
    pass


ANYWHERE = pl.BlockSpec(memory_space=pl.ANY)


def ordered(block, after):
    return call(
        keep_kernel,
        jax.ShapeDtypeStruct(block.shape, block.dtype),
        [],
        limit=2,
        in_specs=[ANYWHERE] * 2,
        out_specs=ANYWHERE,
        input_output_aliases={0: 0},
    )(block, after)


def first_quarter(out_weight):
    core = lax.axis_index("core")
    start = core * HALF + colour(core) * QUARTER
    mine = lax.dynamic_slice_in_dim(out_weight, start, QUARTER, 1)
    below = moved(mine, lambda y, x, z, c: (y, x, z + 1, c))
    above = moved(mine, lambda y, x, z, c: (y, x, z - 1, c))
    far = moved(mine, lambda y, x, z, c: (y, x, z + 2 - 4 * c, c))
    return mine, (below, above, far)


def other_quarters(parts, after):
    block = call(
        join_kernel,
        jax.ShapeDtypeStruct((3 * ROWS, QUARTER), jnp.bfloat16),
        [pltpu.SemaphoreType.DMA((3,))],
        limit=2,
        work=JOIN_WORK,
        in_specs=[ANYWHERE] * 4,
        out_specs=ANYWHERE,
    )(*parts, after)
    upper, lower = block[:SPLIT], block[SPLIT:]
    return [
        block,
        moved(block, lambda y, x, z, c: (y - c, x - 1 + c, z, c)),
        moved(upper, lambda y, x, z, c: (y + 1 - c, x + c, z, c)),
        moved(lower, lambda y, x, z, c: (y - 1 + c, x - c, z, c)),
        moved(block, lambda y, x, z, c: (y + c, x + 1 - c, z, c)),
    ]


def both_halves(blocks, after):
    blocks = blocks[:1] + [ordered(block, after) for block in blocks[1:]]
    return blocks + [moved(block, lambda y, x, z, c: (y, x, z, 1 - c)) for block in blocks]


def project_kernel(columns_ref, own_ref, *refs):
    block_refs, (out_ref, results, out_sem) = refs[:10], refs[10:]
    core, chan = lax.axis_index("core"), lax.axis_index("chan")
    rows = [
        columns_ref[pl.ds(pl.multiple_of((chan + shift) % 4 * ROWS, ROWS), ROWS), :].T
        for shift in (0, 3, 1, 2)
    ]
    own_columns, columns = rows[0], jnp.concatenate(rows[1:], axis=1)
    stores = []
    for half in range(2):
        owner = core if half == 0 else 1 - core
        for step, parts in enumerate(((0,), (1,), (2, 3), (4,))):
            index = 4 * half + step
            start = pl.multiple_of(owner * HALF + (colour(owner) + step) % 4 * QUARTER, QUARTER)
            total = matmul(own_columns, own_ref[:, pl.ds(start, QUARTER)])
            row = 0
            for part in parts:
                block = block_refs[5 * half + part][...]
                total += matmul(columns[:, row : row + block.shape[0]], block)
                row += block.shape[0]
            results[index] = total.astype(jnp.bfloat16)
            store = pltpu.make_async_copy(
                results.at[index], out_ref.at[:, pl.ds(start, QUARTER)], out_sem.at[index]
            )
            store.start()
            stores.append(store)
    for store in stores:
        store.wait()


def body(signal, gate, filter_taps, skip_weight, out_weight):
    mine, parts = first_quarter(out_weight)
    tables = transform_tables()
    packed = call(
        pack_kernel,
        jax.ShapeDtypeStruct((SEQ_DEVICES * 32, LANES), jnp.bfloat16),
        [pltpu.VMEM((SEQ_DEVICES * 32, LANES), jnp.float32)],
        work=PACK_WORK,
        in_specs=[pl.BlockSpec(memory_space=pltpu.VMEM)] * 2 + [ANYWHERE],
    )(signal, filter_taps, mine)
    blocks = other_quarters(parts, packed)
    arrived = lax.all_to_all(
        packed.reshape(SEQ_DEVICES, 32, LANES), AXES, split_axis=0, concat_axis=0, tiled=True
    )
    convolved = call(
        convolve_kernel,
        jax.ShapeDtypeStruct((SEQ_DEVICES * 16, LANES), jnp.bfloat16),
        [
            pltpu.VMEM((SEQ_DEVICES * 32, LANES), jnp.float32),
            pltpu.VMEM((SEQ_DEVICES * 16, LANES), jnp.float32),
        ],
        work=WORK,
    )(arrived.reshape(SEQ_DEVICES * 32, LANES), *tables)
    weights = both_halves(blocks, convolved)
    returned = lax.all_to_all(
        convolved.reshape(SEQ_DEVICES, 16, LANES), AXES, split_axis=0, concat_axis=0, tiled=True
    )
    channels, shard_len = signal.shape
    mixed, rounded = call(
        mix_kernel,
        (
            jax.ShapeDtypeStruct((channels, shard_len), jnp.float32),
            jax.ShapeDtypeStruct((PIECES, channels, LANES), jnp.bfloat16),
        ),
        [pltpu.VMEM((SEQ_DEVICES * 16, LANES), jnp.float32)],
        work=WORK,
    )(returned.reshape(SEQ_DEVICES * 16, LANES), signal, gate, skip_weight[:, None])
    mine = lax.all_to_all(rounded, "chan", split_axis=0, concat_axis=0, tiled=True)
    width = out_weight.shape[1]
    projected = call(
        project_kernel,
        jax.ShapeDtypeStruct((LANES, width), jnp.bfloat16),
        [
            pltpu.VMEM((8, LANES, QUARTER), jnp.bfloat16),
            pltpu.SemaphoreType.DMA((8,)),
        ],
        limit=30,
        in_specs=[pl.BlockSpec(memory_space=pltpu.VMEM)] * 12,
        out_specs=ANYWHERE,
    )(mine.reshape(4 * channels, LANES), out_weight, *weights)
    return mixed, projected


def solution(mesh):
    fine = Mesh(mesh.devices.reshape(4, 4, 2, 2, 4), (*AXES, "chan"))
    slab = P("chan", AXES)
    in_specs = (slab, slab, slab, P("chan"), P("chan", None))
    out_specs = (slab, P((*AXES, "chan"), None))
    return jax.shard_map(body, mesh=fine, in_specs=in_specs, out_specs=out_specs, check_vma=False)
```

```python
import itertools

import jax
import jax.numpy as jnp
import ml_dtypes
import numpy as np
from jax import lax
from jax.experimental import pallas as pl
from jax.experimental.pallas import tpu as pltpu
from jax.sharding import Mesh
from jax.sharding import PartitionSpec as P

AXES = ("y", "x", "zh", "core")
SEQ_DEVICES = 64
ROWS = 256
LANES = 128
POSITIONS = ROWS * LANES
OWN_CHANNELS = 4
PIECES = 4
HALF = 4096
QUARTER = 1024
AHEAD = 3
WORK = 10**11
PACK_WORK = 10**10
JOIN_WORK = 10**10


def transform_tables():
    n1 = (np.arange(SEQ_DEVICES)[None, :] * PIECES + np.arange(PIECES)[:, None]).reshape(-1)
    k1 = np.arange(ROWS) + 0.25
    first = np.exp(-2j * np.pi * np.outer(k1, n1) / ROWS)
    n2 = np.arange(LANES)
    turn = np.exp(-2j * np.pi * np.outer(k1, n2) / POSITIONS)
    second = np.exp(-2j * np.pi * np.outer(n2, n2) / LANES)
    forward_one = np.concatenate([first.real, first.imag], 0)
    forward_two = np.block([[second.real, second.imag], [-second.imag, second.real]])
    back_two = np.block([[second.real, -second.imag], [second.imag, second.real]])
    back_one = np.concatenate([first.real.T, first.imag.T], 1)

    def narrow(table):
        return table.astype(np.float32).astype(ml_dtypes.bfloat16)

    return (
        narrow(forward_one),
        narrow(forward_two),
        narrow(back_two),
        narrow(back_one),
        turn.real.astype(np.float32),
        turn.imag.astype(np.float32),
    )


def pack_kernel(signal_ref, filter_ref, after_ref, out_ref, token_ref, wide):
    for which, source in enumerate((signal_ref, filter_ref)):
        for own in range(OWN_CHANNELS):
            for piece in range(PIECES):
                row = which * 16 + own * PIECES + piece
                wide[pl.ds(row, SEQ_DEVICES, stride=32), :] = source[
                    own * SEQ_DEVICES : (own + 1) * SEQ_DEVICES,
                    piece * LANES : (piece + 1) * LANES,
                ]
    out_ref[...] = wide[...].astype(jnp.bfloat16)
    token_ref[...] = jnp.zeros_like(token_ref)


def matmul(left, right):
    return jnp.dot(left, right, preferred_element_type=jnp.float32)


def convolve_kernel(
    data_ref,
    one_ref,
    two_ref,
    back_two_ref,
    back_one_ref,
    cos_ref,
    sin_ref,
    out_ref,
    token_ref,
    wide,
    result,
):
    wide[...] = data_ref[...].astype(jnp.float32)
    columns = []
    for which in range(2):
        for own in range(OWN_CHANNELS):
            pieces = [
                wide[pl.ds(which * 16 + own * PIECES + piece, SEQ_DEVICES, stride=32), :]
                for piece in range(PIECES)
            ]
            columns.append(jnp.concatenate(pieces, axis=0).astype(jnp.bfloat16))
    turn_cos, turn_sin = cos_ref[...], sin_ref[...]

    def spectrum(column):
        part = matmul(one_ref[...], column)
        real, imag = part[:ROWS], part[ROWS:]
        turned = jnp.concatenate(
            [real * turn_cos - imag * turn_sin, real * turn_sin + imag * turn_cos], axis=1
        )
        both = matmul(turned.astype(jnp.bfloat16), two_ref[...])
        return both[:, :LANES], both[:, LANES:]

    for own in range(OWN_CHANNELS):
        signal_real, signal_imag = spectrum(columns[own])
        filter_real, filter_imag = spectrum(columns[OWN_CHANNELS + own])
        product = jnp.concatenate(
            [
                signal_real * filter_real - signal_imag * filter_imag,
                signal_real * filter_imag + signal_imag * filter_real,
            ],
            axis=1,
        )
        back = matmul(product.astype(jnp.bfloat16), back_two_ref[...])
        real, imag = back[:, :LANES], back[:, LANES:]
        turned = jnp.concatenate(
            [real * turn_cos + imag * turn_sin, imag * turn_cos - real * turn_sin], axis=0
        )
        values = matmul(back_one_ref[...], turned.astype(jnp.bfloat16)) * (1.0 / POSITIONS)
        for piece in range(PIECES):
            result[pl.ds(own * PIECES + piece, SEQ_DEVICES, stride=16), :] = values[
                piece * SEQ_DEVICES : (piece + 1) * SEQ_DEVICES
            ]
    out_ref[...] = result[...].astype(jnp.bfloat16)
    token_ref[...] = jnp.zeros_like(token_ref)


def mix_kernel(conv_ref, signal_ref, gate_ref, skip_ref, mixed_ref, rounded_ref, wide):
    wide[...] = conv_ref[...].astype(jnp.float32)
    for own in range(OWN_CHANNELS):
        rows = slice(own * SEQ_DEVICES, (own + 1) * SEQ_DEVICES)
        skip = skip_ref[rows, :]
        for piece in range(PIECES):
            lanes = slice(piece * LANES, (piece + 1) * LANES)
            conv = wide[pl.ds(own * PIECES + piece, SEQ_DEVICES, stride=16), :]
            mixed = gate_ref[rows, lanes] * (conv + skip * signal_ref[rows, lanes])
            mixed_ref[rows, lanes] = mixed
            rounded_ref[piece, rows, :] = mixed.astype(jnp.bfloat16)


def call(kernel, out_shape, scratch, limit=60, work=0, **options):
    return pl.pallas_call(
        kernel,
        out_shape=out_shape,
        scratch_shapes=scratch,
        compiler_params=pltpu.CompilerParams(vmem_limit_bytes=limit << 20),
        cost_estimate=pl.CostEstimate(flops=work, bytes_accessed=0, transcendentals=0),
        **options,
    )


def device_pairs(move):
    pairs = []
    for y, x, z, core in itertools.product(range(4), range(4), range(8), range(2)):
        spots = []
        for sy, sx, sz, sc in ((y, x, z, core), move(y, x, z, core)):
            sy, sx, sz = sy % 4, sx % 4, sz % 8
            spots.append((((sy * 4 + sx) * 2 + sz // 4) * 2 + sc) * 4 + sz % 4)
        pairs.append(tuple(spots))
    return pairs


def moved(array, move):
    return lax.ppermute(array, (*AXES, "chan"), device_pairs(move))


def colour(core):
    x, y = lax.axis_index("x"), lax.axis_index("y")
    return jnp.where(core == 0, x + 2 * y, 2 * x + y) % 4


def join_kernel(below_ref, above_ref, far_ref, after_ref, out_ref, sem):
    copies = [
        pltpu.make_async_copy(ref, out_ref.at[pl.ds(index * ROWS, ROWS)], sem.at[index])
        for index, ref in enumerate((below_ref, above_ref, far_ref))
    ]
    for copy in copies:
        copy.start()
    for copy in copies:
        copy.wait()


def keep_kernel(block_ref, after_ref, out_ref):
    pass


ANYWHERE = pl.BlockSpec(memory_space=pl.ANY)
TOKEN = jax.ShapeDtypeStruct((8, LANES), jnp.float32)


def ordered(block, after):
    return call(
        keep_kernel,
        jax.ShapeDtypeStruct(block.shape, block.dtype),
        [],
        limit=2,
        in_specs=[ANYWHERE] * 2,
        out_specs=ANYWHERE,
        input_output_aliases={0: 0},
    )(block, after)


def first_quarter(out_weight):
    core = lax.axis_index("core")
    start = core * HALF + colour(core) * QUARTER
    mine = lax.dynamic_slice_in_dim(out_weight, start, QUARTER, 1)
    below = moved(mine, lambda y, x, z, c: (y, x, z + 1, c))
    above = moved(mine, lambda y, x, z, c: (y, x, z - 1, c))
    far = moved(mine, lambda y, x, z, c: (y, x, z + 2 - 4 * c, c))
    return mine, (below, above, far)


def other_quarters(parts, after):
    block = call(
        join_kernel,
        jax.ShapeDtypeStruct((3 * ROWS, QUARTER), jnp.bfloat16),
        [pltpu.SemaphoreType.DMA((3,))],
        limit=2,
        work=JOIN_WORK,
        in_specs=[ANYWHERE] * 4,
        out_specs=ANYWHERE,
    )(*parts, after)
    return [
        block,
        moved(block, lambda y, x, z, c: (y - c, x - 1 + c, z, c)),
        moved(block, lambda y, x, z, c: (y + 1 - c, x + c, z, c)),
        moved(block, lambda y, x, z, c: (y + c, x + 1 - c, z, c)),
    ]


def both_halves(blocks, after):
    blocks = blocks[:1] + [ordered(block, after) for block in blocks[1:]]
    return blocks + [moved(block, lambda y, x, z, c: (y, x, z, 1 - c)) for block in blocks]


def project_kernel(columns_ref, own_ref, *refs):
    block_refs, (out_ref, weights, results, own_sem, block_sem, out_sem) = refs[:8], refs[8:]
    core, chan = lax.axis_index("core"), lax.axis_index("chan")
    starts, loads = [], []
    for index, block_ref in enumerate(block_refs):
        owner = core if index < 4 else 1 - core
        start = pl.multiple_of(owner * HALF + (colour(owner) + index) % 4 * QUARTER, QUARTER)
        slot = index % (AHEAD + 1)
        starts.append(start)
        loads.append(
            (
                pltpu.make_async_copy(
                    own_ref.at[:, pl.ds(start, QUARTER)],
                    weights.at[slot, pl.ds(0, ROWS)],
                    own_sem.at[index],
                ),
                pltpu.make_async_copy(
                    block_ref, weights.at[slot, pl.ds(ROWS, 3 * ROWS)], block_sem.at[index]
                ),
            )
        )
    for index in range(AHEAD):
        for load in loads[index]:
            load.start()
    rows = [
        columns_ref[pl.ds(pl.multiple_of((chan + shift) % 4 * ROWS, ROWS), ROWS), :].T
        for shift in (0, 3, 1, 2)
    ]
    left = jnp.concatenate(rows, axis=1)
    stores = []
    for index in range(8):
        for load in loads[index]:
            load.wait()
        if index + AHEAD < 8:
            for load in loads[index + AHEAD]:
                load.start()
        results[index] = matmul(left, weights[index % (AHEAD + 1)]).astype(jnp.bfloat16)
        store = pltpu.make_async_copy(
            results.at[index], out_ref.at[:, pl.ds(starts[index], QUARTER)], out_sem.at[index]
        )
        store.start()
        stores.append(store)
    for store in stores:
        store.wait()


def body(signal, gate, filter_taps, skip_weight, out_weight):
    mine, parts = first_quarter(out_weight)
    tables = transform_tables()
    packed, packed_token = call(
        pack_kernel,
        (jax.ShapeDtypeStruct((SEQ_DEVICES * 32, LANES), jnp.bfloat16), TOKEN),
        [pltpu.VMEM((SEQ_DEVICES * 32, LANES), jnp.float32)],
        work=PACK_WORK,
        in_specs=[pl.BlockSpec(memory_space=pltpu.VMEM)] * 2 + [ANYWHERE],
    )(signal, filter_taps, mine)
    blocks = other_quarters(parts, packed_token)
    arrived = lax.all_to_all(
        packed.reshape(SEQ_DEVICES, 32, LANES), AXES, split_axis=0, concat_axis=0, tiled=True
    )
    convolved, convolved_token = call(
        convolve_kernel,
        (jax.ShapeDtypeStruct((SEQ_DEVICES * 16, LANES), jnp.bfloat16), TOKEN),
        [
            pltpu.VMEM((SEQ_DEVICES * 32, LANES), jnp.float32),
            pltpu.VMEM((SEQ_DEVICES * 16, LANES), jnp.float32),
        ],
        work=WORK,
    )(arrived.reshape(SEQ_DEVICES * 32, LANES), *tables)
    weights = both_halves(blocks, convolved_token)
    returned = lax.all_to_all(
        convolved.reshape(SEQ_DEVICES, 16, LANES), AXES, split_axis=0, concat_axis=0, tiled=True
    )
    channels, shard_len = signal.shape
    mixed, rounded = call(
        mix_kernel,
        (
            jax.ShapeDtypeStruct((channels, shard_len), jnp.float32),
            jax.ShapeDtypeStruct((PIECES, channels, LANES), jnp.bfloat16),
        ),
        [pltpu.VMEM((SEQ_DEVICES * 16, LANES), jnp.float32)],
        work=WORK,
    )(returned.reshape(SEQ_DEVICES * 16, LANES), signal, gate, skip_weight[:, None])
    mine = lax.all_to_all(rounded, "chan", split_axis=0, concat_axis=0, tiled=True)
    width = out_weight.shape[1]
    projected = call(
        project_kernel,
        jax.ShapeDtypeStruct((LANES, width), jnp.bfloat16),
        [
            pltpu.VMEM((AHEAD + 1, 4 * ROWS, QUARTER), jnp.bfloat16),
            pltpu.VMEM((8, LANES, QUARTER), jnp.bfloat16),
            pltpu.SemaphoreType.DMA((8,)),
            pltpu.SemaphoreType.DMA((8,)),
            pltpu.SemaphoreType.DMA((8,)),
        ],
        in_specs=[pl.BlockSpec(memory_space=pltpu.VMEM)] + [ANYWHERE] * 9,
        out_specs=ANYWHERE,
    )(mine.reshape(4 * channels, LANES), out_weight, *weights)
    return mixed, projected


def solution(mesh):
    fine = Mesh(mesh.devices.reshape(4, 4, 2, 2, 4), (*AXES, "chan"))
    slab = P("chan", AXES)
    in_specs = (slab, slab, slab, P("chan"), P("chan", None))
    out_specs = (slab, P((*AXES, "chan"), None))
    return jax.shard_map(body, mesh=fine, in_specs=in_specs, out_specs=out_specs, check_vma=False)
```

```python
import itertools

import jax
import jax.numpy as jnp
import ml_dtypes
import numpy as np
from jax import lax
from jax.experimental import pallas as pl
from jax.experimental.pallas import tpu as pltpu
from jax.sharding import Mesh
from jax.sharding import PartitionSpec as P

AXES = ("y", "x", "zh", "core")
SEQ_DEVICES = 64
ROWS = 256
LANES = 128
POSITIONS = ROWS * LANES
OWN_CHANNELS = 4
PIECES = 4
HALF = 4096
QUARTER = 1024
LAST = 48
WORK = 10**11
PACK_WORK = 10**10
JOIN_WORK = 10**10


def transform_tables():
    n1 = (np.arange(SEQ_DEVICES)[None, :] * PIECES + np.arange(PIECES)[:, None]).reshape(-1)
    k1 = np.arange(ROWS) + 0.25
    first = np.exp(-2j * np.pi * np.outer(k1, n1) / ROWS)
    n2 = np.arange(LANES)
    turn = np.exp(-2j * np.pi * np.outer(k1, n2) / POSITIONS)
    second = np.exp(-2j * np.pi * np.outer(n2, n2) / LANES)
    forward_one = np.concatenate([first.real, first.imag], 0)
    forward_two = np.block([[second.real, second.imag], [-second.imag, second.real]])
    back_two = np.block([[second.real, -second.imag], [second.imag, second.real]])
    back_one = np.concatenate([first.real.T, first.imag.T], 1)

    def narrow(table):
        return table.astype(np.float32).astype(ml_dtypes.bfloat16)

    return (
        narrow(forward_one),
        narrow(forward_two),
        narrow(back_two),
        narrow(back_one),
        turn.real.astype(np.float32),
        turn.imag.astype(np.float32),
    )


def pack_kernel(signal_ref, filter_ref, after_ref, out_ref, token_ref, wide):
    for which, source in enumerate((signal_ref, filter_ref)):
        for own in range(OWN_CHANNELS):
            for piece in range(PIECES):
                row = which * 16 + own * PIECES + piece
                wide[pl.ds(row, SEQ_DEVICES, stride=32), :] = source[
                    own * SEQ_DEVICES : (own + 1) * SEQ_DEVICES,
                    piece * LANES : (piece + 1) * LANES,
                ]
    out_ref[...] = wide[...].astype(jnp.bfloat16)
    token_ref[...] = jnp.zeros_like(token_ref)


def matmul(left, right):
    return jnp.dot(left, right, preferred_element_type=jnp.float32)


def convolve_kernel(
    data_ref,
    one_ref,
    two_ref,
    back_two_ref,
    back_one_ref,
    cos_ref,
    sin_ref,
    out_ref,
    token_ref,
    wide,
    result,
):
    wide[...] = data_ref[...].astype(jnp.float32)
    columns = []
    for which in range(2):
        for own in range(OWN_CHANNELS):
            pieces = [
                wide[pl.ds(which * 16 + own * PIECES + piece, SEQ_DEVICES, stride=32), :]
                for piece in range(PIECES)
            ]
            columns.append(jnp.concatenate(pieces, axis=0).astype(jnp.bfloat16))
    turn_cos, turn_sin = cos_ref[...], sin_ref[...]

    def spectrum(column):
        part = matmul(one_ref[...], column)
        real, imag = part[:ROWS], part[ROWS:]
        turned = jnp.concatenate(
            [real * turn_cos - imag * turn_sin, real * turn_sin + imag * turn_cos], axis=1
        )
        both = matmul(turned.astype(jnp.bfloat16), two_ref[...])
        return both[:, :LANES], both[:, LANES:]

    for own in range(OWN_CHANNELS):
        signal_real, signal_imag = spectrum(columns[own])
        filter_real, filter_imag = spectrum(columns[OWN_CHANNELS + own])
        product = jnp.concatenate(
            [
                signal_real * filter_real - signal_imag * filter_imag,
                signal_real * filter_imag + signal_imag * filter_real,
            ],
            axis=1,
        )
        back = matmul(product.astype(jnp.bfloat16), back_two_ref[...])
        real, imag = back[:, :LANES], back[:, LANES:]
        turned = jnp.concatenate(
            [real * turn_cos + imag * turn_sin, imag * turn_cos - real * turn_sin], axis=0
        )
        values = matmul(back_one_ref[...], turned.astype(jnp.bfloat16)) * (1.0 / POSITIONS)
        for piece in range(PIECES):
            result[pl.ds(own * PIECES + piece, SEQ_DEVICES, stride=16), :] = values[
                piece * SEQ_DEVICES : (piece + 1) * SEQ_DEVICES
            ]
    out_ref[...] = result[...].astype(jnp.bfloat16)
    token_ref[...] = jnp.zeros_like(token_ref)


def mix_kernel(conv_ref, signal_ref, gate_ref, skip_ref, mixed_ref, rounded_ref, wide):
    wide[...] = conv_ref[...].astype(jnp.float32)
    for own in range(OWN_CHANNELS):
        rows = slice(own * SEQ_DEVICES, (own + 1) * SEQ_DEVICES)
        skip = skip_ref[rows, :]
        for piece in range(PIECES):
            lanes = slice(piece * LANES, (piece + 1) * LANES)
            conv = wide[pl.ds(own * PIECES + piece, SEQ_DEVICES, stride=16), :]
            mixed = gate_ref[rows, lanes] * (conv + skip * signal_ref[rows, lanes])
            mixed_ref[rows, lanes] = mixed
            rounded_ref[piece, rows, :] = mixed.astype(jnp.bfloat16)


def call(kernel, out_shape, scratch, limit=60, work=0, **options):
    return pl.pallas_call(
        kernel,
        out_shape=out_shape,
        scratch_shapes=scratch,
        compiler_params=pltpu.CompilerParams(vmem_limit_bytes=limit << 20),
        cost_estimate=pl.CostEstimate(flops=work, bytes_accessed=0, transcendentals=0),
        **options,
    )


def device_pairs(move):
    pairs = []
    for y, x, z, core in itertools.product(range(4), range(4), range(8), range(2)):
        spots = []
        for sy, sx, sz, sc in ((y, x, z, core), move(y, x, z, core)):
            sy, sx, sz = sy % 4, sx % 4, sz % 8
            spots.append((((sy * 4 + sx) * 2 + sz // 4) * 2 + sc) * 4 + sz % 4)
        pairs.append(tuple(spots))
    return pairs


def moved(array, move):
    return lax.ppermute(array, (*AXES, "chan"), device_pairs(move))


def colour(core):
    x, y = lax.axis_index("x"), lax.axis_index("y")
    return jnp.where(core == 0, x + 2 * y, 2 * x + y) % 4


def join_kernel(below_ref, above_ref, after_ref, out_ref, sem):
    copies = [
        pltpu.make_async_copy(ref, out_ref.at[pl.ds(index * ROWS, ROWS)], sem.at[index])
        for index, ref in enumerate((below_ref, above_ref))
    ]
    for copy in copies:
        copy.start()
    for copy in copies:
        copy.wait()


def keep_kernel(block_ref, after_ref, out_ref):
    pass


ANYWHERE = pl.BlockSpec(memory_space=pl.ANY)
TOKEN = jax.ShapeDtypeStruct((8, LANES), jnp.float32)


def ordered(block, after):
    return call(
        keep_kernel,
        jax.ShapeDtypeStruct(block.shape, block.dtype),
        [],
        limit=2,
        in_specs=[ANYWHERE] * 2,
        out_specs=ANYWHERE,
        input_output_aliases={0: 0},
    )(block, after)


def first_quarter(out_weight):
    core = lax.axis_index("core")
    start = core * HALF + colour(core) * QUARTER
    mine = lax.dynamic_slice_in_dim(out_weight, start, QUARTER, 1)
    below = moved(mine, lambda y, x, z, c: (y, x, z + 1, c))
    above = moved(mine, lambda y, x, z, c: (y, x, z - 1, c))
    far = moved(mine, lambda y, x, z, c: (y, x, z + 2 - 4 * c, c))
    return mine, (below, above, far)


def joined(below, above, after):
    return call(
        join_kernel,
        jax.ShapeDtypeStruct((2 * ROWS, QUARTER), jnp.bfloat16),
        [pltpu.SemaphoreType.DMA((2,))],
        limit=2,
        work=JOIN_WORK,
        in_specs=[ANYWHERE] * 3,
        out_specs=ANYWHERE,
    )(below, above, after)


def other_quarters(block, way):
    return [
        block,
        moved(block, lambda y, x, z, c: (y - c, x - 1 + c, z, c)),
        moved(block, lambda y, x, z, c: (y + way * (1 - c), x + way * c, z, c)),
        moved(block, lambda y, x, z, c: (y + c, x + 1 - c, z, c)),
    ]


def project_kernel(mine_ref, theirs_ref, own_ref, *refs):
    near_refs, far_refs = refs[:4], refs[4:8]
    out_ref, for_them_ref, own, results, own_sem, out_sem = refs[8:]
    core, chan = lax.axis_index("core"), lax.axis_index("chan")
    first = core * HALF
    load = pltpu.make_async_copy(own_ref.at[:, pl.ds(pl.multiple_of(first, HALF), HALF)], own, own_sem)
    load.start()
    rows = [
        jnp.concatenate(
            [
                ref[pl.ds(pl.multiple_of((chan + shift) % 4 * ROWS, ROWS), ROWS), :].T
                for ref in (mine_ref, theirs_ref)
            ],
            axis=0,
        )
        for shift in (0, 3, 1, 2)
    ]
    own_columns, near_columns, far_columns = rows[0], jnp.concatenate(rows[1:3], axis=1), rows[3]
    load.wait()
    stores = []
    for index in range(4):
        start = pl.multiple_of((colour(core) + index) % 4 * QUARTER, QUARTER)
        total = matmul(own_columns, own[:, pl.ds(start, QUARTER)])
        total += matmul(near_columns, near_refs[index][...])
        total += matmul(far_columns, far_refs[index][...])
        results[index] = total.astype(jnp.bfloat16)
        for rank, (target, offset) in enumerate(((out_ref, first + start), (for_them_ref, start))):
            store = pltpu.make_async_copy(
                results.at[index, pl.ds(rank * LANES, LANES)],
                target.at[:, pl.ds(pl.multiple_of(offset, QUARTER), QUARTER)],
                out_sem.at[index, rank],
            )
            store.start()
            stores.append(store)
    for store in stores:
        store.wait()


def fill_kernel(half_ref, from_them_ref, out_ref, sem):
    start = pl.multiple_of((1 - lax.axis_index("core")) * HALF, HALF)
    copy = pltpu.make_async_copy(from_them_ref, out_ref.at[:, pl.ds(start, HALF)], sem)
    copy.start()
    copy.wait()


def swapped(array):
    return moved(array, lambda y, x, z, c: (y, x, z, 1 - c))


def body(signal, gate, filter_taps, skip_weight, out_weight):
    mine, (below, above, far) = first_quarter(out_weight)
    tables = transform_tables()
    packed, packed_token = call(
        pack_kernel,
        (jax.ShapeDtypeStruct((SEQ_DEVICES * 32, LANES), jnp.bfloat16), TOKEN),
        [pltpu.VMEM((SEQ_DEVICES * 32, LANES), jnp.float32)],
        work=PACK_WORK,
        in_specs=[pl.BlockSpec(memory_space=pltpu.VMEM)] * 2 + [ANYWHERE],
    )(signal, filter_taps, mine)
    near = other_quarters(joined(below, above, packed_token), 1)
    far = other_quarters(far, -1)
    arrived = lax.all_to_all(
        packed.reshape(SEQ_DEVICES, 32, LANES), AXES, split_axis=0, concat_axis=0, tiled=True
    )
    convolved, convolved_token = call(
        convolve_kernel,
        (jax.ShapeDtypeStruct((SEQ_DEVICES * 16, LANES), jnp.bfloat16), TOKEN),
        [
            pltpu.VMEM((SEQ_DEVICES * 32, LANES), jnp.float32),
            pltpu.VMEM((SEQ_DEVICES * 16, LANES), jnp.float32),
        ],
        work=WORK,
    )(arrived.reshape(SEQ_DEVICES * 32, LANES), *tables)
    returned = lax.all_to_all(
        convolved.reshape(SEQ_DEVICES, 16, LANES), AXES, split_axis=0, concat_axis=0, tiled=True
    )
    channels, shard_len = signal.shape
    mixed, rounded = call(
        mix_kernel,
        (
            jax.ShapeDtypeStruct((channels, shard_len), jnp.float32),
            jax.ShapeDtypeStruct((PIECES, channels, LANES), jnp.bfloat16),
        ),
        [pltpu.VMEM((SEQ_DEVICES * 16, LANES), jnp.float32)],
        work=WORK,
    )(returned.reshape(SEQ_DEVICES * 16, LANES), signal, gate, skip_weight[:, None])
    mine = lax.all_to_all(rounded, "chan", split_axis=0, concat_axis=0, tiled=True)
    mine = mine.reshape(4 * channels, LANES)
    half_filled, for_them = call(
        project_kernel,
        (
            jax.ShapeDtypeStruct((LANES, 2 * HALF), jnp.bfloat16),
            jax.ShapeDtypeStruct((LANES, HALF), jnp.bfloat16),
        ),
        [
            pltpu.VMEM((ROWS, HALF), jnp.bfloat16),
            pltpu.VMEM((4, 2 * LANES, QUARTER), jnp.bfloat16),
            pltpu.SemaphoreType.DMA(()),
            pltpu.SemaphoreType.DMA((4, 2)),
        ],
        limit=LAST,
        in_specs=[pl.BlockSpec(memory_space=pltpu.VMEM)] * 2
        + [ANYWHERE]
        + [pl.BlockSpec(memory_space=pltpu.VMEM)] * 8,
        out_specs=(ANYWHERE, ANYWHERE),
    )(mine, swapped(mine), out_weight, *near, *far)
    projected = call(
        fill_kernel,
        jax.ShapeDtypeStruct(half_filled.shape, half_filled.dtype),
        [pltpu.SemaphoreType.DMA(())],
        limit=2,
        in_specs=[ANYWHERE] * 2,
        out_specs=ANYWHERE,
        input_output_aliases={0: 0},
    )(half_filled, swapped(for_them))
    return mixed, projected


def solution(mesh):
    fine = Mesh(mesh.devices.reshape(4, 4, 2, 2, 4), (*AXES, "chan"))
    slab = P("chan", AXES)
    in_specs = (slab, slab, slab, P("chan"), P("chan", None))
    out_specs = (slab, P((*AXES, "chan"), None))
    return jax.shard_map(body, mesh=fine, in_specs=in_specs, out_specs=out_specs, check_vma=False)
```

```python
import itertools

import jax
import jax.numpy as jnp
import ml_dtypes
import numpy as np
from jax import lax
from jax.experimental import pallas as pl
from jax.experimental.pallas import tpu as pltpu
from jax.sharding import Mesh
from jax.sharding import PartitionSpec as P

AXES = ("y", "x", "zh", "core")
SEQ_DEVICES = 64
ROWS = 256
LANES = 128
POSITIONS = ROWS * LANES
OWN_CHANNELS = 4
PIECES = 4
HALF = 4096
QUARTER = 1024
LAST = 48
WORK = 10**11
PACK_WORK = 10**10


def transform_tables():
    n1 = (np.arange(SEQ_DEVICES)[None, :] * PIECES + np.arange(PIECES)[:, None]).reshape(-1)
    k1 = np.arange(ROWS) + 0.25
    first = np.exp(-2j * np.pi * np.outer(k1, n1) / ROWS)
    n2 = np.arange(LANES)
    turn = np.exp(-2j * np.pi * np.outer(k1, n2) / POSITIONS)
    second = np.exp(-2j * np.pi * np.outer(n2, n2) / LANES)
    forward_one = np.concatenate([first.real, first.imag], 0)
    forward_two = np.block([[second.real, second.imag], [-second.imag, second.real]])
    back_two = np.block([[second.real, -second.imag], [second.imag, second.real]])
    back_one = np.concatenate([first.real.T, first.imag.T], 1)

    def narrow(table):
        return table.astype(np.float32).astype(ml_dtypes.bfloat16)

    return (
        narrow(forward_one),
        narrow(forward_two),
        narrow(back_two),
        narrow(back_one),
        turn.real.astype(np.float32),
        turn.imag.astype(np.float32),
    )


def pack_kernel(signal_ref, filter_ref, after_ref, out_ref, token_ref, wide):
    for which, source in enumerate((signal_ref, filter_ref)):
        for own in range(OWN_CHANNELS):
            for piece in range(PIECES):
                row = which * 16 + own * PIECES + piece
                wide[pl.ds(row, SEQ_DEVICES, stride=32), :] = source[
                    own * SEQ_DEVICES : (own + 1) * SEQ_DEVICES,
                    piece * LANES : (piece + 1) * LANES,
                ]
    out_ref[...] = wide[...].astype(jnp.bfloat16)


def matmul(left, right):
    return jnp.dot(left, right, preferred_element_type=jnp.float32)


def convolve_kernel(
    data_ref,
    one_ref,
    two_ref,
    back_two_ref,
    back_one_ref,
    cos_ref,
    sin_ref,
    out_ref,
    wide,
    result,
):
    wide[...] = data_ref[...].astype(jnp.float32)
    columns = []
    for which in range(2):
        for own in range(OWN_CHANNELS):
            pieces = [
                wide[pl.ds(which * 16 + own * PIECES + piece, SEQ_DEVICES, stride=32), :]
                for piece in range(PIECES)
            ]
            columns.append(jnp.concatenate(pieces, axis=0).astype(jnp.bfloat16))
    turn_cos, turn_sin = cos_ref[...], sin_ref[...]

    def spectrum(column):
        part = matmul(one_ref[...], column)
        real, imag = part[:ROWS], part[ROWS:]
        turned = jnp.concatenate(
            [real * turn_cos - imag * turn_sin, real * turn_sin + imag * turn_cos], axis=1
        )
        both = matmul(turned.astype(jnp.bfloat16), two_ref[...])
        return both[:, :LANES], both[:, LANES:]

    for own in range(OWN_CHANNELS):
        signal_real, signal_imag = spectrum(columns[own])
        filter_real, filter_imag = spectrum(columns[OWN_CHANNELS + own])
        product = jnp.concatenate(
            [
                signal_real * filter_real - signal_imag * filter_imag,
                signal_real * filter_imag + signal_imag * filter_real,
            ],
            axis=1,
        )
        back = matmul(product.astype(jnp.bfloat16), back_two_ref[...])
        real, imag = back[:, :LANES], back[:, LANES:]
        turned = jnp.concatenate(
            [real * turn_cos + imag * turn_sin, imag * turn_cos - real * turn_sin], axis=0
        )
        values = matmul(back_one_ref[...], turned.astype(jnp.bfloat16)) * (1.0 / POSITIONS)
        for piece in range(PIECES):
            result[pl.ds(own * PIECES + piece, SEQ_DEVICES, stride=16), :] = values[
                piece * SEQ_DEVICES : (piece + 1) * SEQ_DEVICES
            ]
    out_ref[...] = result[...].astype(jnp.bfloat16)


def mix_kernel(conv_ref, signal_ref, gate_ref, skip_ref, mixed_ref, rounded_ref, wide):
    wide[...] = conv_ref[...].astype(jnp.float32)
    for own in range(OWN_CHANNELS):
        rows = slice(own * SEQ_DEVICES, (own + 1) * SEQ_DEVICES)
        skip = skip_ref[rows, :]
        for piece in range(PIECES):
            lanes = slice(piece * LANES, (piece + 1) * LANES)
            conv = wide[pl.ds(own * PIECES + piece, SEQ_DEVICES, stride=16), :]
            mixed = gate_ref[rows, lanes] * (conv + skip * signal_ref[rows, lanes])
            mixed_ref[rows, lanes] = mixed
            rounded_ref[piece, rows, :] = mixed.astype(jnp.bfloat16)


def call(kernel, out_shape, scratch, limit=60, work=0, **options):
    return pl.pallas_call(
        kernel,
        out_shape=out_shape,
        scratch_shapes=scratch,
        compiler_params=pltpu.CompilerParams(vmem_limit_bytes=limit << 20),
        cost_estimate=pl.CostEstimate(flops=work, bytes_accessed=0, transcendentals=0),
        **options,
    )


def device_pairs(move):
    pairs = []
    for y, x, z, core in itertools.product(range(4), range(4), range(8), range(2)):
        spots = []
        for sy, sx, sz, sc in ((y, x, z, core), move(y, x, z, core)):
            sy, sx, sz = sy % 4, sx % 4, sz % 8
            spots.append((((sy * 4 + sx) * 2 + sz // 4) * 2 + sc) * 4 + sz % 4)
        pairs.append(tuple(spots))
    return pairs


def moved(array, move):
    return lax.ppermute(array, (*AXES, "chan"), device_pairs(move))


def colour(core):
    x, y = lax.axis_index("x"), lax.axis_index("y")
    return jnp.where(core == 0, x + 2 * y, 2 * x + y) % 4


def join_kernel(below_ref, above_ref, after_ref, out_ref, token_ref, sem):
    copies = [
        pltpu.make_async_copy(ref, out_ref.at[pl.ds(index * ROWS, ROWS)], sem.at[index])
        for index, ref in enumerate((below_ref, above_ref))
    ]
    for copy in copies:
        copy.start()
    for copy in copies:
        copy.wait()


def keep_kernel(block_ref, *refs):
    pass


ANYWHERE = pl.BlockSpec(memory_space=pl.ANY)
TOKEN = jax.ShapeDtypeStruct((8, LANES), jnp.float32)


def ordered(block, *after):
    return call(
        keep_kernel,
        jax.ShapeDtypeStruct(block.shape, block.dtype),
        [],
        in_specs=[ANYWHERE] * (1 + len(after)),
        out_specs=ANYWHERE,
        input_output_aliases={0: 0},
    )(block, *after)


def nothing_kernel(*refs):
    pass


def token_of(*blocks):
    return call(
        nothing_kernel, TOKEN, [], limit=2, in_specs=[ANYWHERE] * len(blocks), out_specs=ANYWHERE
    )(*blocks)


def first_quarter(out_weight):
    core = lax.axis_index("core")
    start = core * HALF + colour(core) * QUARTER
    mine = lax.dynamic_slice_in_dim(out_weight, start, QUARTER, 1)
    below = moved(mine, lambda y, x, z, c: (y, x, z + 1, c))
    above = moved(mine, lambda y, x, z, c: (y, x, z - 1, c))
    return mine, below, above


def joined(below, above, after):
    return call(
        join_kernel,
        (jax.ShapeDtypeStruct((2 * ROWS, QUARTER), jnp.bfloat16), TOKEN),
        [pltpu.SemaphoreType.DMA((2,))],
        limit=2,
        in_specs=[ANYWHERE] * 3,
        out_specs=(ANYWHERE, ANYWHERE),
    )(below, above, after)


def other_quarters(block, way):
    return [
        block,
        moved(block, lambda y, x, z, c: (y - c, x - 1 + c, z, c)),
        moved(block, lambda y, x, z, c: (y + way * (1 - c), x + way * c, z, c)),
        moved(block, lambda y, x, z, c: (y + c, x + 1 - c, z, c)),
    ]


def project_kernel(mine_ref, theirs_ref, own_ref, *refs):
    near_refs, far_refs = refs[:4], refs[4:8]
    out_ref, for_them_ref, own, results, own_sem, out_sem = refs[8:]
    core, chan = lax.axis_index("core"), lax.axis_index("chan")
    first = core * HALF
    load = pltpu.make_async_copy(own_ref.at[:, pl.ds(pl.multiple_of(first, HALF), HALF)], own, own_sem)
    load.start()
    rows = [
        jnp.concatenate(
            [
                ref[pl.ds(pl.multiple_of((chan + shift) % 4 * ROWS, ROWS), ROWS), :].T
                for ref in (mine_ref, theirs_ref)
            ],
            axis=0,
        )
        for shift in (0, 3, 1, 2)
    ]
    own_columns, near_columns, far_columns = rows[0], jnp.concatenate(rows[1:3], axis=1), rows[3]
    load.wait()
    stores = []
    for index in range(4):
        start = pl.multiple_of((colour(core) + index) % 4 * QUARTER, QUARTER)
        for tile in range(0, QUARTER, ROWS):
            lanes = slice(tile, tile + ROWS)
            total = matmul(own_columns, own[:, pl.ds(pl.multiple_of(start + tile, ROWS), ROWS)])
            total += matmul(near_columns, near_refs[index][:, lanes])
            total += matmul(far_columns, far_refs[index][:, lanes])
            results[index, :, lanes] = total.astype(jnp.bfloat16)
        for rank, (target, offset) in enumerate(((out_ref, first + start), (for_them_ref, start))):
            store = pltpu.make_async_copy(
                results.at[index, pl.ds(rank * LANES, LANES)],
                target.at[:, pl.ds(pl.multiple_of(offset, QUARTER), QUARTER)],
                out_sem.at[index, rank],
            )
            store.start()
            stores.append(store)
    for store in stores:
        store.wait()


def fill_kernel(half_ref, from_them_ref, out_ref, sem):
    start = pl.multiple_of((1 - lax.axis_index("core")) * HALF, HALF)
    copy = pltpu.make_async_copy(from_them_ref, out_ref.at[:, pl.ds(start, HALF)], sem)
    copy.start()
    copy.wait()


def swapped(array):
    return moved(array, lambda y, x, z, c: (y, x, z, 1 - c))


def body(signal, gate, filter_taps, skip_weight, out_weight):
    mine, below, above = first_quarter(out_weight)
    tables = transform_tables()
    packed, packed_token = call(
        pack_kernel,
        (jax.ShapeDtypeStruct((SEQ_DEVICES * 32, LANES), jnp.bfloat16), TOKEN),
        [pltpu.VMEM((SEQ_DEVICES * 32, LANES), jnp.float32)],
        work=PACK_WORK,
        in_specs=[pl.BlockSpec(memory_space=pltpu.VMEM)] * 2 + [ANYWHERE],
        out_specs=(pl.BlockSpec(memory_space=pltpu.VMEM), ANYWHERE),
    )(signal, filter_taps, mine)
    near, near_token = joined(below, above, packed_token)
    packed = ordered(packed, near_token)
    near = other_quarters(near, 1)
    far = moved(ordered(mine, near_token), lambda y, x, z, c: (y, x, z + 2 - 4 * c, c))
    arrived = lax.all_to_all(
        packed.reshape(SEQ_DEVICES, 32, LANES), AXES, split_axis=0, concat_axis=0, tiled=True
    )
    convolved = call(
        convolve_kernel,
        jax.ShapeDtypeStruct((SEQ_DEVICES * 16, LANES), jnp.bfloat16),
        [
            pltpu.VMEM((SEQ_DEVICES * 32, LANES), jnp.float32),
            pltpu.VMEM((SEQ_DEVICES * 16, LANES), jnp.float32),
        ],
        work=WORK,
    )(arrived.reshape(SEQ_DEVICES * 32, LANES), *tables)
    convolved = ordered(convolved, token_of(far, *near[1:]))
    far = other_quarters(far, -1)
    returned = lax.all_to_all(
        convolved.reshape(SEQ_DEVICES, 16, LANES), AXES, split_axis=0, concat_axis=0, tiled=True
    )
    returned = returned.reshape(SEQ_DEVICES * 16, LANES)
    channels, shard_len = signal.shape
    mixed, rounded = call(
        mix_kernel,
        (
            jax.ShapeDtypeStruct((channels, shard_len), jnp.float32),
            jax.ShapeDtypeStruct((PIECES, channels, LANES), jnp.bfloat16),
        ),
        [pltpu.VMEM((SEQ_DEVICES * 16, LANES), jnp.float32)],
        work=WORK,
    )(returned, signal, gate, skip_weight[:, None])
    rounded = ordered(rounded, token_of(*far[1:]))
    mine = lax.all_to_all(rounded, "chan", split_axis=0, concat_axis=0, tiled=True)
    mine = mine.reshape(4 * channels, LANES)
    half_filled, for_them = call(
        project_kernel,
        (
            jax.ShapeDtypeStruct((LANES, 2 * HALF), jnp.bfloat16),
            jax.ShapeDtypeStruct((LANES, HALF), jnp.bfloat16),
        ),
        [
            pltpu.VMEM((ROWS, HALF), jnp.bfloat16),
            pltpu.VMEM((4, 2 * LANES, QUARTER), jnp.bfloat16),
            pltpu.SemaphoreType.DMA(()),
            pltpu.SemaphoreType.DMA((4, 2)),
        ],
        limit=LAST,
        in_specs=[pl.BlockSpec(memory_space=pltpu.VMEM)] * 2
        + [ANYWHERE]
        + [pl.BlockSpec(memory_space=pltpu.VMEM)] * 8,
        out_specs=(ANYWHERE, ANYWHERE),
    )(mine, swapped(mine), out_weight, *near, *far)
    projected = call(
        fill_kernel,
        jax.ShapeDtypeStruct(half_filled.shape, half_filled.dtype),
        [pltpu.SemaphoreType.DMA(())],
        limit=2,
        in_specs=[ANYWHERE] * 2,
        out_specs=ANYWHERE,
        input_output_aliases={0: 0},
    )(half_filled, swapped(for_them))
    return mixed, projected


def solution(mesh):
    fine = Mesh(mesh.devices.reshape(4, 4, 2, 2, 4), (*AXES, "chan"))
    slab = P("chan", AXES)
    in_specs = (slab, slab, slab, P("chan"), P("chan", None))
    out_specs = (slab, P((*AXES, "chan"), None))
    return jax.shard_map(body, mesh=fine, in_specs=in_specs, out_specs=out_specs, check_vma=False)
```

```python
import itertools

import jax
import jax.numpy as jnp
import ml_dtypes
import numpy as np
from jax import lax
from jax.experimental import pallas as pl
from jax.experimental.pallas import tpu as pltpu
from jax.sharding import Mesh
from jax.sharding import PartitionSpec as P

AXES = ("y", "x", "zh", "core")
SEQ_DEVICES = 64
ROWS = 256
LANES = 128
POSITIONS = ROWS * LANES
OWN_CHANNELS = 4
PIECES = 4
HALF = 4096
QUARTER = 1024
SPLIT = 384
CONVOLVE = 60
MIX = 24
LAST = 30
WORK = 10**11
PACK_WORK = 10**10
JOIN_WORK = 10**10


def transform_tables():
    n1 = (np.arange(SEQ_DEVICES)[None, :] * PIECES + np.arange(PIECES)[:, None]).reshape(-1)
    k1 = np.arange(ROWS) + 0.25
    first = np.exp(-2j * np.pi * np.outer(k1, n1) / ROWS)
    n2 = np.arange(LANES)
    turn = np.exp(-2j * np.pi * np.outer(k1, n2) / POSITIONS)
    second = np.exp(-2j * np.pi * np.outer(n2, n2) / LANES)
    forward_one = np.concatenate([first.real, first.imag], 0)
    forward_two = np.block([[second.real, second.imag], [-second.imag, second.real]])
    back_two = np.block([[second.real, -second.imag], [second.imag, second.real]])
    back_one = np.concatenate([first.real.T, first.imag.T], 1)

    def narrow(table):
        return table.astype(np.float32).astype(ml_dtypes.bfloat16)

    left, right = np.split(back_one, 2, axis=1)
    factors = np.concatenate([forward_one, forward_two, back_two, left, right], 0)
    return narrow(factors), np.concatenate([turn.real, turn.imag], 0).astype(np.float32)


def pack_kernel(signal_ref, filter_ref, after_ref, out_ref, token_ref, wide):
    for which, source in enumerate((signal_ref, filter_ref)):
        for own in range(OWN_CHANNELS):
            for piece in range(PIECES):
                row = which * 16 + own * PIECES + piece
                wide[pl.ds(row, SEQ_DEVICES, stride=32), :] = source[
                    own * SEQ_DEVICES : (own + 1) * SEQ_DEVICES,
                    piece * LANES : (piece + 1) * LANES,
                ]
    out_ref[...] = wide[...].astype(jnp.bfloat16)


def matmul(left, right):
    return jnp.dot(left, right, preferred_element_type=jnp.float32)


def convolve_kernel(data_ref, factors_ref, turn_ref, out_ref, token_ref, wide, result):
    forward_one = factors_ref[: 2 * ROWS]
    forward_two, back_two, back_left, back_right = (
        factors_ref[row * ROWS : (row + 1) * ROWS] for row in range(2, 6)
    )
    wide[...] = data_ref[...].astype(jnp.float32)
    columns = []
    for which in range(2):
        for own in range(OWN_CHANNELS):
            pieces = [
                wide[pl.ds(which * 16 + own * PIECES + piece, SEQ_DEVICES, stride=32), :]
                for piece in range(PIECES)
            ]
            columns.append(jnp.concatenate(pieces, axis=0).astype(jnp.bfloat16))
    turn_cos, turn_sin = turn_ref[:ROWS], turn_ref[ROWS:]

    def spectrum(column):
        part = matmul(forward_one, column)
        real, imag = part[:ROWS], part[ROWS:]
        turned = jnp.concatenate(
            [real * turn_cos - imag * turn_sin, real * turn_sin + imag * turn_cos], axis=1
        )
        both = matmul(turned.astype(jnp.bfloat16), forward_two)
        return both[:, :LANES], both[:, LANES:]

    for own in range(OWN_CHANNELS):
        signal_real, signal_imag = spectrum(columns[own])
        filter_real, filter_imag = spectrum(columns[OWN_CHANNELS + own])
        product = jnp.concatenate(
            [
                signal_real * filter_real - signal_imag * filter_imag,
                signal_real * filter_imag + signal_imag * filter_real,
            ],
            axis=1,
        )
        back = matmul(product.astype(jnp.bfloat16), back_two)
        real, imag = back[:, :LANES], back[:, LANES:]
        turned_real = (real * turn_cos + imag * turn_sin).astype(jnp.bfloat16)
        turned_imag = (imag * turn_cos - real * turn_sin).astype(jnp.bfloat16)
        values = matmul(back_left, turned_real) + matmul(back_right, turned_imag)
        values = values * (1.0 / POSITIONS)
        for piece in range(PIECES):
            result[pl.ds(own * PIECES + piece, SEQ_DEVICES, stride=16), :] = values[
                piece * SEQ_DEVICES : (piece + 1) * SEQ_DEVICES
            ]
    out_ref[...] = result[...].astype(jnp.bfloat16)


def mix_kernel(conv_ref, signal_ref, gate_ref, skip_ref, mixed_ref, rounded_ref, wide):
    wide[...] = conv_ref[...].astype(jnp.float32)
    for own in range(OWN_CHANNELS):
        rows = slice(own * SEQ_DEVICES, (own + 1) * SEQ_DEVICES)
        skip = skip_ref[rows, :]
        for piece in range(PIECES):
            lanes = slice(piece * LANES, (piece + 1) * LANES)
            conv = wide[pl.ds(own * PIECES + piece, SEQ_DEVICES, stride=16), :]
            mixed = gate_ref[rows, lanes] * (conv + skip * signal_ref[rows, lanes])
            mixed_ref[rows, lanes] = mixed
            rounded_ref[piece, rows, :] = mixed.astype(jnp.bfloat16)


def call(kernel, out_shape, scratch, limit=60, work=0, **options):
    return pl.pallas_call(
        kernel,
        out_shape=out_shape,
        scratch_shapes=scratch,
        compiler_params=pltpu.CompilerParams(vmem_limit_bytes=limit << 20),
        cost_estimate=pl.CostEstimate(flops=work, bytes_accessed=0, transcendentals=0),
        **options,
    )


def device_pairs(move):
    pairs = []
    for y, x, z, core in itertools.product(range(4), range(4), range(8), range(2)):
        spots = []
        for sy, sx, sz, sc in ((y, x, z, core), move(y, x, z, core)):
            sy, sx, sz = sy % 4, sx % 4, sz % 8
            spots.append((((sy * 4 + sx) * 2 + sz // 4) * 2 + sc) * 4 + sz % 4)
        pairs.append(tuple(spots))
    return pairs


def moved(array, move):
    return lax.ppermute(array, (*AXES, "chan"), device_pairs(move))


def colour(core):
    x, y = lax.axis_index("x"), lax.axis_index("y")
    return jnp.where(core == 0, x + 2 * y, 2 * x + y) % 4


def join_kernel(below_ref, above_ref, far_ref, after_ref, out_ref, sem):
    copies = [
        pltpu.make_async_copy(ref, out_ref.at[pl.ds(index * ROWS, ROWS)], sem.at[index])
        for index, ref in enumerate((below_ref, above_ref, far_ref))
    ]
    for copy in copies:
        copy.start()
    for copy in copies:
        copy.wait()


def keep_kernel(block_ref, after_ref, out_ref):
    pass


ANYWHERE = pl.BlockSpec(memory_space=pl.ANY)
INSIDE = pl.BlockSpec(memory_space=pltpu.VMEM)
TOKEN = jax.ShapeDtypeStruct((8, LANES), jnp.float32)


def ordered(block, after):
    return call(
        keep_kernel,
        jax.ShapeDtypeStruct(block.shape, block.dtype),
        [],
        limit=2,
        in_specs=[ANYWHERE] * 2,
        out_specs=ANYWHERE,
        input_output_aliases={0: 0},
    )(block, after)


def first_quarter(out_weight):
    core = lax.axis_index("core")
    start = core * HALF + colour(core) * QUARTER
    mine = lax.dynamic_slice_in_dim(out_weight, start, QUARTER, 1)
    below = moved(mine, lambda y, x, z, c: (y, x, z + 1, c))
    above = moved(mine, lambda y, x, z, c: (y, x, z - 1, c))
    far = moved(mine, lambda y, x, z, c: (y, x, z + 2 - 4 * c, c))
    return mine, (below, above, far)


def other_quarters(parts, after):
    block = call(
        join_kernel,
        jax.ShapeDtypeStruct((3 * ROWS, QUARTER), jnp.bfloat16),
        [pltpu.SemaphoreType.DMA((3,))],
        limit=2,
        work=JOIN_WORK,
        in_specs=[ANYWHERE] * 4,
        out_specs=ANYWHERE,
    )(*parts, after)
    upper, lower = block[:SPLIT], block[SPLIT:]
    return [
        block,
        moved(block, lambda y, x, z, c: (y - c, x - 1 + c, z, c)),
        moved(upper, lambda y, x, z, c: (y + 1 - c, x + c, z, c)),
        moved(lower, lambda y, x, z, c: (y - 1 + c, x - c, z, c)),
        moved(block, lambda y, x, z, c: (y + c, x + 1 - c, z, c)),
    ]


def both_halves(blocks, after):
    blocks = blocks[:1] + [ordered(block, after) for block in blocks[1:]]
    return blocks + [moved(block, lambda y, x, z, c: (y, x, z, 1 - c)) for block in blocks]


def project_kernel(columns_ref, own_ref, *refs):
    block_refs, (out_ref, results, out_sem) = refs[:10], refs[10:]
    core, chan = lax.axis_index("core"), lax.axis_index("chan")
    rows = [
        columns_ref[pl.ds(pl.multiple_of((chan + shift) % 4 * ROWS, ROWS), ROWS), :].T
        for shift in (0, 3, 1, 2)
    ]
    own_columns, columns = rows[0], jnp.concatenate(rows[1:], axis=1)
    stores = []
    for half in range(2):
        owner = core if half == 0 else 1 - core
        for step, parts in enumerate(((0,), (1,), (2, 3), (4,))):
            index = 4 * half + step
            start = pl.multiple_of(owner * HALF + (colour(owner) + step) % 4 * QUARTER, QUARTER)
            total = matmul(own_columns, own_ref[:, pl.ds(start, QUARTER)])
            row = 0
            for part in parts:
                block = block_refs[5 * half + part][...]
                total += matmul(columns[:, row : row + block.shape[0]], block)
                row += block.shape[0]
            results[index] = total.astype(jnp.bfloat16)
            store = pltpu.make_async_copy(
                results.at[index], out_ref.at[:, pl.ds(start, QUARTER)], out_sem.at[index]
            )
            store.start()
            stores.append(store)
    for store in stores:
        store.wait()


def body(signal, gate, filter_taps, skip_weight, out_weight):
    mine, parts = first_quarter(out_weight)
    tables = transform_tables()
    packed, packed_token = call(
        pack_kernel,
        (jax.ShapeDtypeStruct((SEQ_DEVICES * 32, LANES), jnp.bfloat16), TOKEN),
        [pltpu.VMEM((SEQ_DEVICES * 32, LANES), jnp.float32)],
        work=PACK_WORK,
        in_specs=[INSIDE] * 2 + [ANYWHERE],
        out_specs=(INSIDE, ANYWHERE),
    )(signal, filter_taps, mine)
    blocks = other_quarters(parts, packed_token)
    arrived = lax.all_to_all(
        packed.reshape(SEQ_DEVICES, 32, LANES), AXES, split_axis=0, concat_axis=0, tiled=True
    )
    convolved, convolved_token = call(
        convolve_kernel,
        (jax.ShapeDtypeStruct((SEQ_DEVICES * 16, LANES), jnp.bfloat16), TOKEN),
        [
            pltpu.VMEM((SEQ_DEVICES * 32, LANES), jnp.float32),
            pltpu.VMEM((SEQ_DEVICES * 16, LANES), jnp.float32),
        ],
        limit=CONVOLVE,
        in_specs=[INSIDE] * 3,
        out_specs=(INSIDE, ANYWHERE),
        work=WORK,
    )(arrived.reshape(SEQ_DEVICES * 32, LANES), *tables)
    weights = both_halves(blocks, convolved_token)
    returned = lax.all_to_all(
        convolved.reshape(SEQ_DEVICES, 16, LANES), AXES, split_axis=0, concat_axis=0, tiled=True
    )
    channels, shard_len = signal.shape
    mixed, rounded = call(
        mix_kernel,
        (
            jax.ShapeDtypeStruct((channels, shard_len), jnp.float32),
            jax.ShapeDtypeStruct((PIECES, channels, LANES), jnp.bfloat16),
        ),
        [pltpu.VMEM((SEQ_DEVICES * 16, LANES), jnp.float32)],
        limit=MIX,
        work=WORK,
    )(returned.reshape(SEQ_DEVICES * 16, LANES), signal, gate, skip_weight[:, None])
    mine = lax.all_to_all(rounded, "chan", split_axis=0, concat_axis=0, tiled=True)
    width = out_weight.shape[1]
    projected = call(
        project_kernel,
        jax.ShapeDtypeStruct((LANES, width), jnp.bfloat16),
        [
            pltpu.VMEM((8, LANES, QUARTER), jnp.bfloat16),
            pltpu.SemaphoreType.DMA((8,)),
        ],
        limit=LAST,
        in_specs=[INSIDE] * 12,
        out_specs=ANYWHERE,
    )(mine.reshape(4 * channels, LANES), out_weight, *weights)
    return mixed, projected


def solution(mesh):
    fine = Mesh(mesh.devices.reshape(4, 4, 2, 2, 4), (*AXES, "chan"))
    slab = P("chan", AXES)
    in_specs = (slab, slab, slab, P("chan"), P("chan", None))
    out_specs = (slab, P((*AXES, "chan"), None))
    return jax.shard_map(body, mesh=fine, in_specs=in_specs, out_specs=out_specs, check_vma=False)
```

```python
import itertools

import jax
import jax.numpy as jnp
import ml_dtypes
import numpy as np
from jax import lax
from jax.experimental import pallas as pl
from jax.experimental.pallas import tpu as pltpu
from jax.sharding import Mesh
from jax.sharding import PartitionSpec as P

AXES = ("y", "x", "zh", "core")
SEQ_DEVICES = 64
ROWS = 256
LANES = 128
POSITIONS = ROWS * LANES
OWN_CHANNELS = 4
PIECES = 4
HALF = 4096
QUARTER = 1024
SPLIT = 384
CONVOLVE = 60
MIX = 24
LAST = 30
WORK = 10**11
PACK_WORK = 10**10
JOIN_WORK = 10**10


def transform_tables():
    n1 = (np.arange(SEQ_DEVICES)[None, :] * PIECES + np.arange(PIECES)[:, None]).reshape(-1)
    k1 = np.arange(ROWS) + 0.25
    first = np.exp(-2j * np.pi * np.outer(k1, n1) / ROWS)
    n2 = np.arange(LANES)
    turn = np.exp(-2j * np.pi * np.outer(k1, n2) / POSITIONS)
    second = np.exp(-2j * np.pi * np.outer(n2, n2) / LANES)
    forward_one = np.concatenate([first.real, first.imag], 0)
    forward_two = np.block([[second.real, second.imag], [-second.imag, second.real]])
    back_two = np.block([[second.real, -second.imag], [second.imag, second.real]])
    back_one = np.concatenate([first.real.T, first.imag.T], 1)

    def narrow(table):
        return table.astype(np.float32).astype(ml_dtypes.bfloat16)

    left, right = np.split(back_one, 2, axis=1)
    factors = np.concatenate([forward_one, forward_two, back_two, left, right], 0)
    return narrow(factors), np.concatenate([turn.real, turn.imag], 0).astype(np.float32)


def pack_kernel(signal_ref, filter_ref, out_ref, token_ref, wide):
    for which, source in enumerate((signal_ref, filter_ref)):
        for own in range(OWN_CHANNELS):
            for piece in range(PIECES):
                row = which * 16 + own * PIECES + piece
                wide[pl.ds(row, SEQ_DEVICES, stride=32), :] = source[
                    own * SEQ_DEVICES : (own + 1) * SEQ_DEVICES,
                    piece * LANES : (piece + 1) * LANES,
                ]
    out_ref[...] = wide[...].astype(jnp.bfloat16)


def matmul(left, right):
    return jnp.dot(left, right, preferred_element_type=jnp.float32)


def convolve_kernel(data_ref, factors_ref, turn_ref, out_ref, wide, result):
    forward_one = factors_ref[: 2 * ROWS]
    forward_two, back_two, back_left, back_right = (
        factors_ref[row * ROWS : (row + 1) * ROWS] for row in range(2, 6)
    )
    wide[...] = data_ref[...].astype(jnp.float32)
    columns = []
    for which in range(2):
        for own in range(OWN_CHANNELS):
            pieces = [
                wide[pl.ds(which * 16 + own * PIECES + piece, SEQ_DEVICES, stride=32), :]
                for piece in range(PIECES)
            ]
            columns.append(jnp.concatenate(pieces, axis=0).astype(jnp.bfloat16))
    turn_cos, turn_sin = turn_ref[:ROWS], turn_ref[ROWS:]

    def spectrum(column):
        part = matmul(forward_one, column)
        real, imag = part[:ROWS], part[ROWS:]
        turned = jnp.concatenate(
            [real * turn_cos - imag * turn_sin, real * turn_sin + imag * turn_cos], axis=1
        )
        both = matmul(turned.astype(jnp.bfloat16), forward_two)
        return both[:, :LANES], both[:, LANES:]

    for own in range(OWN_CHANNELS):
        signal_real, signal_imag = spectrum(columns[own])
        filter_real, filter_imag = spectrum(columns[OWN_CHANNELS + own])
        product = jnp.concatenate(
            [
                signal_real * filter_real - signal_imag * filter_imag,
                signal_real * filter_imag + signal_imag * filter_real,
            ],
            axis=1,
        )
        back = matmul(product.astype(jnp.bfloat16), back_two)
        real, imag = back[:, :LANES], back[:, LANES:]
        turned_real = (real * turn_cos + imag * turn_sin).astype(jnp.bfloat16)
        turned_imag = (imag * turn_cos - real * turn_sin).astype(jnp.bfloat16)
        values = matmul(back_left, turned_real) + matmul(back_right, turned_imag)
        values = values * (1.0 / POSITIONS)
        for piece in range(PIECES):
            result[pl.ds(own * PIECES + piece, SEQ_DEVICES, stride=16), :] = values[
                piece * SEQ_DEVICES : (piece + 1) * SEQ_DEVICES
            ]
    out_ref[...] = result[...].astype(jnp.bfloat16)


def mix_kernel(conv_ref, signal_ref, gate_ref, skip_ref, mixed_ref, rounded_ref, wide):
    wide[...] = conv_ref[...].astype(jnp.float32)
    for own in range(OWN_CHANNELS):
        rows = slice(own * SEQ_DEVICES, (own + 1) * SEQ_DEVICES)
        skip = skip_ref[rows, :]
        for piece in range(PIECES):
            lanes = slice(piece * LANES, (piece + 1) * LANES)
            conv = wide[pl.ds(own * PIECES + piece, SEQ_DEVICES, stride=16), :]
            mixed = gate_ref[rows, lanes] * (conv + skip * signal_ref[rows, lanes])
            mixed_ref[rows, lanes] = mixed
            rounded_ref[piece, rows, :] = mixed.astype(jnp.bfloat16)


def call(kernel, out_shape, scratch, limit=60, work=0, **options):
    return pl.pallas_call(
        kernel,
        out_shape=out_shape,
        scratch_shapes=scratch,
        compiler_params=pltpu.CompilerParams(vmem_limit_bytes=limit << 20),
        cost_estimate=pl.CostEstimate(flops=work, bytes_accessed=0, transcendentals=0),
        **options,
    )


def device_pairs(move):
    pairs = []
    for y, x, z, core in itertools.product(range(4), range(4), range(8), range(2)):
        spots = []
        for sy, sx, sz, sc in ((y, x, z, core), move(y, x, z, core)):
            sy, sx, sz = sy % 4, sx % 4, sz % 8
            spots.append((((sy * 4 + sx) * 2 + sz // 4) * 2 + sc) * 4 + sz % 4)
        pairs.append(tuple(spots))
    return pairs


def moved(array, move):
    return lax.ppermute(array, (*AXES, "chan"), device_pairs(move))


def colour(core):
    x, y = lax.axis_index("x"), lax.axis_index("y")
    return jnp.where(core == 0, x + 2 * y, 2 * x + y) % 4


def join_kernel(below_ref, above_ref, far_ref, after_ref, out_ref, sem):
    copies = [
        pltpu.make_async_copy(ref, out_ref.at[pl.ds(index * ROWS, ROWS)], sem.at[index])
        for index, ref in enumerate((below_ref, above_ref, far_ref))
    ]
    for copy in copies:
        copy.start()
    for copy in copies:
        copy.wait()


ANYWHERE = pl.BlockSpec(memory_space=pl.ANY)
INSIDE = pl.BlockSpec(memory_space=pltpu.VMEM)
TOKEN = jax.ShapeDtypeStruct((8, LANES), jnp.float32)


def first_quarter(out_weight):
    core = lax.axis_index("core")
    start = core * HALF + colour(core) * QUARTER
    mine = lax.dynamic_slice_in_dim(out_weight, start, QUARTER, 1)
    below = moved(mine, lambda y, x, z, c: (y, x, z + 1, c))
    above = moved(mine, lambda y, x, z, c: (y, x, z - 1, c))
    far = moved(mine, lambda y, x, z, c: (y, x, z + 2 - 4 * c, c))
    return below, above, far


def other_quarters(parts, after):
    block = call(
        join_kernel,
        jax.ShapeDtypeStruct((3 * ROWS, QUARTER), jnp.bfloat16),
        [pltpu.SemaphoreType.DMA((3,))],
        limit=2,
        work=JOIN_WORK,
        in_specs=[ANYWHERE] * 4,
        out_specs=ANYWHERE,
    )(*parts, after)
    upper, lower = block[:SPLIT], block[SPLIT:]
    return [
        block,
        moved(block, lambda y, x, z, c: (y - c, x - 1 + c, z, c)),
        moved(upper, lambda y, x, z, c: (y + 1 - c, x + c, z, c)),
        moved(lower, lambda y, x, z, c: (y - 1 + c, x - c, z, c)),
        moved(block, lambda y, x, z, c: (y + c, x + 1 - c, z, c)),
    ]


def project_kernel(mine_ref, theirs_ref, own_ref, *refs):
    block_refs, (out_ref, for_them_ref, results, out_sem) = refs[:5], refs[5:]
    core, chan = lax.axis_index("core"), lax.axis_index("chan")
    first = core * HALF
    rows = [
        jnp.concatenate(
            [
                ref[pl.ds(pl.multiple_of((chan + shift) % 4 * ROWS, ROWS), ROWS), :].T
                for ref in (mine_ref, theirs_ref)
            ],
            axis=0,
        )
        for shift in (0, 3, 1, 2)
    ]
    own_columns, columns = rows[0], jnp.concatenate(rows[1:], axis=1)
    stores = []
    for index, parts in enumerate(((0,), (1,), (2, 3), (4,))):
        start = pl.multiple_of((colour(core) + index) % 4 * QUARTER, QUARTER)
        place = pl.multiple_of(first + start, QUARTER)
        total = matmul(own_columns, own_ref[:, pl.ds(place, QUARTER)])
        row = 0
        for part in parts:
            block = block_refs[part][...]
            total += matmul(columns[:, row : row + block.shape[0]], block)
            row += block.shape[0]
        results[index] = total.astype(jnp.bfloat16)
        for rank, (target, offset) in enumerate(((out_ref, place), (for_them_ref, start))):
            store = pltpu.make_async_copy(
                results.at[index, pl.ds(rank * LANES, LANES)],
                target.at[:, pl.ds(offset, QUARTER)],
                out_sem.at[index, rank],
            )
            store.start()
            stores.append(store)
    for store in stores:
        store.wait()


def fill_kernel(half_ref, from_them_ref, out_ref, sem):
    start = pl.multiple_of((1 - lax.axis_index("core")) * HALF, HALF)
    copy = pltpu.make_async_copy(from_them_ref, out_ref.at[:, pl.ds(start, HALF)], sem)
    copy.start()
    copy.wait()


def swapped(array):
    return moved(array, lambda y, x, z, c: (y, x, z, 1 - c))


def body(signal, gate, filter_taps, skip_weight, out_weight):
    parts = first_quarter(out_weight)
    tables = transform_tables()
    packed, packed_token = call(
        pack_kernel,
        (jax.ShapeDtypeStruct((SEQ_DEVICES * 32, LANES), jnp.bfloat16), TOKEN),
        [pltpu.VMEM((SEQ_DEVICES * 32, LANES), jnp.float32)],
        work=PACK_WORK,
        in_specs=[INSIDE] * 2,
        out_specs=(INSIDE, ANYWHERE),
    )(signal, filter_taps)
    blocks = other_quarters(parts, packed_token)
    arrived = lax.all_to_all(
        packed.reshape(SEQ_DEVICES, 32, LANES), AXES, split_axis=0, concat_axis=0, tiled=True
    )
    convolved = call(
        convolve_kernel,
        jax.ShapeDtypeStruct((SEQ_DEVICES * 16, LANES), jnp.bfloat16),
        [
            pltpu.VMEM((SEQ_DEVICES * 32, LANES), jnp.float32),
            pltpu.VMEM((SEQ_DEVICES * 16, LANES), jnp.float32),
        ],
        limit=CONVOLVE,
        work=WORK,
    )(arrived.reshape(SEQ_DEVICES * 32, LANES), *tables)
    returned = lax.all_to_all(
        convolved.reshape(SEQ_DEVICES, 16, LANES), AXES, split_axis=0, concat_axis=0, tiled=True
    )
    channels, shard_len = signal.shape
    mixed, rounded = call(
        mix_kernel,
        (
            jax.ShapeDtypeStruct((channels, shard_len), jnp.float32),
            jax.ShapeDtypeStruct((PIECES, channels, LANES), jnp.bfloat16),
        ),
        [pltpu.VMEM((SEQ_DEVICES * 16, LANES), jnp.float32)],
        limit=MIX,
        work=WORK,
    )(returned.reshape(SEQ_DEVICES * 16, LANES), signal, gate, skip_weight[:, None])
    mine = lax.all_to_all(rounded, "chan", split_axis=0, concat_axis=0, tiled=True)
    mine = mine.reshape(4 * channels, LANES)
    half_filled, for_them = call(
        project_kernel,
        (
            jax.ShapeDtypeStruct((LANES, 2 * HALF), jnp.bfloat16),
            jax.ShapeDtypeStruct((LANES, HALF), jnp.bfloat16),
        ),
        [
            pltpu.VMEM((4, 2 * LANES, QUARTER), jnp.bfloat16),
            pltpu.SemaphoreType.DMA((4, 2)),
        ],
        limit=LAST,
        in_specs=[INSIDE] * 8,
        out_specs=(ANYWHERE, ANYWHERE),
    )(mine, swapped(mine), out_weight, *blocks)
    projected = call(
        fill_kernel,
        jax.ShapeDtypeStruct(half_filled.shape, half_filled.dtype),
        [pltpu.SemaphoreType.DMA(())],
        limit=2,
        in_specs=[ANYWHERE] * 2,
        out_specs=ANYWHERE,
        input_output_aliases={0: 0},
    )(half_filled, swapped(for_them))
    return mixed, projected


def solution(mesh):
    fine = Mesh(mesh.devices.reshape(4, 4, 2, 2, 4), (*AXES, "chan"))
    slab = P("chan", AXES)
    in_specs = (slab, slab, slab, P("chan"), P("chan", None))
    out_specs = (slab, P((*AXES, "chan"), None))
    return jax.shard_map(body, mesh=fine, in_specs=in_specs, out_specs=out_specs, check_vma=False)
```

```python
import functools
import itertools

import jax
import jax.numpy as jnp
import ml_dtypes
import numpy as np
from jax import lax
from jax.experimental import pallas as pl
from jax.experimental.pallas import tpu as pltpu
from jax.sharding import Mesh
from jax.sharding import PartitionSpec as P

AXES = ("y", "x", "zh", "core")
SEQ_DEVICES = 64
ROWS = 256
LANES = 128
POSITIONS = ROWS * LANES
OWN_CHANNELS = 4
PIECES = 4
HALF = 4096
QUARTER = 1024
SPLIT = 384
CONVOLVE = 60
MIX = 24
LAST = 48
WORK = 10**11
PACK_WORK = 10**10
JOIN_WORK = 10**10


def transform_tables():
    n1 = (np.arange(SEQ_DEVICES)[None, :] * PIECES + np.arange(PIECES)[:, None]).reshape(-1)
    k1 = np.arange(ROWS) + 0.25
    first = np.exp(-2j * np.pi * np.outer(k1, n1) / ROWS)
    n2 = np.arange(LANES)
    turn = np.exp(-2j * np.pi * np.outer(k1, n2) / POSITIONS)
    second = np.exp(-2j * np.pi * np.outer(n2, n2) / LANES)
    forward_one = np.concatenate([first.real, first.imag], 0)
    forward_two = np.block([[second.real, second.imag], [-second.imag, second.real]])
    back_two = np.block([[second.real, -second.imag], [second.imag, second.real]])
    back_one = np.concatenate([first.real.T, first.imag.T], 1)

    def narrow(table):
        return table.astype(np.float32).astype(ml_dtypes.bfloat16)

    left, right = np.split(back_one, 2, axis=1)
    factors = np.concatenate([forward_one, forward_two, back_two, left, right], 0)
    return narrow(factors), np.concatenate([turn.real, turn.imag], 0).astype(np.float32)


def pack_kernel(signal_ref, filter_ref, out_ref, token_ref, wide):
    for which, source in enumerate((signal_ref, filter_ref)):
        for own in range(OWN_CHANNELS):
            for piece in range(PIECES):
                row = which * 16 + own * PIECES + piece
                wide[pl.ds(row, SEQ_DEVICES, stride=32), :] = source[
                    own * SEQ_DEVICES : (own + 1) * SEQ_DEVICES,
                    piece * LANES : (piece + 1) * LANES,
                ]
    out_ref[...] = wide[...].astype(jnp.bfloat16)


def matmul(left, right):
    return jnp.dot(left, right, preferred_element_type=jnp.float32)


def convolve_kernel(data_ref, factors_ref, turn_ref, out_ref, wide, result):
    forward_one = factors_ref[: 2 * ROWS]
    forward_two, back_two, back_left, back_right = (
        factors_ref[row * ROWS : (row + 1) * ROWS] for row in range(2, 6)
    )
    wide[...] = data_ref[...].astype(jnp.float32)
    columns = []
    for which in range(2):
        for own in range(OWN_CHANNELS):
            pieces = [
                wide[pl.ds(which * 16 + own * PIECES + piece, SEQ_DEVICES, stride=32), :]
                for piece in range(PIECES)
            ]
            columns.append(jnp.concatenate(pieces, axis=0).astype(jnp.bfloat16))
    turn_cos, turn_sin = turn_ref[:ROWS], turn_ref[ROWS:]

    def spectrum(column):
        part = matmul(forward_one, column)
        real, imag = part[:ROWS], part[ROWS:]
        turned = jnp.concatenate(
            [real * turn_cos - imag * turn_sin, real * turn_sin + imag * turn_cos], axis=1
        )
        both = matmul(turned.astype(jnp.bfloat16), forward_two)
        return both[:, :LANES], both[:, LANES:]

    for own in range(OWN_CHANNELS):
        signal_real, signal_imag = spectrum(columns[own])
        filter_real, filter_imag = spectrum(columns[OWN_CHANNELS + own])
        product = jnp.concatenate(
            [
                signal_real * filter_real - signal_imag * filter_imag,
                signal_real * filter_imag + signal_imag * filter_real,
            ],
            axis=1,
        )
        back = matmul(product.astype(jnp.bfloat16), back_two)
        real, imag = back[:, :LANES], back[:, LANES:]
        turned_real = (real * turn_cos + imag * turn_sin).astype(jnp.bfloat16)
        turned_imag = (imag * turn_cos - real * turn_sin).astype(jnp.bfloat16)
        values = matmul(back_left, turned_real) + matmul(back_right, turned_imag)
        values = values * (1.0 / POSITIONS)
        for piece in range(PIECES):
            result[pl.ds(own * PIECES + piece, SEQ_DEVICES, stride=16), :] = values[
                piece * SEQ_DEVICES : (piece + 1) * SEQ_DEVICES
            ]
    out_ref[...] = result[...].astype(jnp.bfloat16)


def mix_kernel(conv_ref, signal_ref, gate_ref, skip_ref, mixed_ref, rounded_ref, wide):
    wide[...] = conv_ref[...].astype(jnp.float32)
    for own in range(OWN_CHANNELS):
        rows = slice(own * SEQ_DEVICES, (own + 1) * SEQ_DEVICES)
        skip = skip_ref[rows, :]
        for piece in range(PIECES):
            lanes = slice(piece * LANES, (piece + 1) * LANES)
            conv = wide[pl.ds(own * PIECES + piece, SEQ_DEVICES, stride=16), :]
            mixed = gate_ref[rows, lanes] * (conv + skip * signal_ref[rows, lanes])
            mixed_ref[rows, lanes] = mixed
            rounded_ref[piece, rows, :] = mixed.astype(jnp.bfloat16)


def call(kernel, out_shape, scratch, limit=60, work=0, **options):
    return pl.pallas_call(
        kernel,
        out_shape=out_shape,
        scratch_shapes=scratch,
        compiler_params=pltpu.CompilerParams(vmem_limit_bytes=limit << 20),
        cost_estimate=pl.CostEstimate(flops=work, bytes_accessed=0, transcendentals=0),
        **options,
    )


def device_pairs(move):
    pairs = []
    for y, x, z, core in itertools.product(range(4), range(4), range(8), range(2)):
        spots = []
        for sy, sx, sz, sc in ((y, x, z, core), move(y, x, z, core)):
            sy, sx, sz = sy % 4, sx % 4, sz % 8
            spots.append((((sy * 4 + sx) * 2 + sz // 4) * 2 + sc) * 4 + sz % 4)
        pairs.append(tuple(spots))
    return pairs


def moved(array, move):
    return lax.ppermute(array, (*AXES, "chan"), device_pairs(move))


def colour(core):
    x, y = lax.axis_index("x"), lax.axis_index("y")
    return jnp.where(core == 0, x + 2 * y, 2 * x + y) % 4


def join_kernel(below_ref, above_ref, far_ref, after_ref, out_ref, sem):
    copies = [
        pltpu.make_async_copy(ref, out_ref.at[pl.ds(index * ROWS, ROWS)], sem.at[index])
        for index, ref in enumerate((below_ref, above_ref, far_ref))
    ]
    for copy in copies:
        copy.start()
    for copy in copies:
        copy.wait()


ANYWHERE = pl.BlockSpec(memory_space=pl.ANY)
INSIDE = pl.BlockSpec(memory_space=pltpu.VMEM)
TOKEN = jax.ShapeDtypeStruct((8, LANES), jnp.float32)


def first_quarter(out_weight):
    core = lax.axis_index("core")
    start = core * HALF + colour(core) * QUARTER
    mine = lax.dynamic_slice_in_dim(out_weight, start, QUARTER, 1)
    below = moved(mine, lambda y, x, z, c: (y, x, z + 1, c))
    above = moved(mine, lambda y, x, z, c: (y, x, z - 1, c))
    far = moved(mine, lambda y, x, z, c: (y, x, z + 2 - 4 * c, c))
    return below, above, far


def other_quarters(parts, after):
    block = call(
        join_kernel,
        jax.ShapeDtypeStruct((3 * ROWS, QUARTER), jnp.bfloat16),
        [pltpu.SemaphoreType.DMA((3,))],
        limit=2,
        work=JOIN_WORK,
        in_specs=[ANYWHERE] * 4,
        out_specs=ANYWHERE,
    )(*parts, after)
    upper, lower = block[:SPLIT], block[SPLIT:]
    return [
        block,
        moved(block, lambda y, x, z, c: (y - c, x - 1 + c, z, c)),
        moved(upper, lambda y, x, z, c: (y + 1 - c, x + c, z, c)),
        moved(lower, lambda y, x, z, c: (y - 1 + c, x - c, z, c)),
        moved(block, lambda y, x, z, c: (y + c, x + 1 - c, z, c)),
    ]


def place_of(core, index):
    return pl.multiple_of(core * HALF + (colour(core) + index) % 4 * QUARTER, QUARTER)


def project_kernel(quarters, mine_ref, theirs_ref, own_ref, *refs):
    count = sum(parts for _, parts in quarters)
    block_refs, (out_ref, for_them_ref, own, results, own_sem, out_sem) = refs[:count], refs[-6:]
    core, chan = lax.axis_index("core"), lax.axis_index("chan")
    loads = [
        pltpu.make_async_copy(
            own_ref.at[:, pl.ds(place_of(core, index), QUARTER)], own.at[order], own_sem.at[order]
        )
        for order, (index, _) in enumerate(quarters)
    ]
    for load in loads:
        load.start()
    rows = [
        jnp.concatenate(
            [
                ref[pl.ds(pl.multiple_of((chan + shift) % 4 * ROWS, ROWS), ROWS), :].T
                for ref in (mine_ref, theirs_ref)
            ],
            axis=0,
        )
        for shift in (0, 3, 1, 2)
    ]
    own_columns, columns = rows[0], jnp.concatenate(rows[1:], axis=1)
    stores, part = [], 0
    for order, (index, parts) in enumerate(quarters):
        place = place_of(core, index)
        loads[order].wait()
        total = matmul(own_columns, own[order])
        row = 0
        for block_ref in block_refs[part : part + parts]:
            block = block_ref[...]
            total += matmul(columns[:, row : row + block.shape[0]], block)
            row += block.shape[0]
        part += parts
        results[order] = total.astype(jnp.bfloat16)
        targets = (
            out_ref.at[:, pl.ds(place, QUARTER)],
            for_them_ref.at[:, pl.ds(order * QUARTER, QUARTER)],
        )
        for rank, target in enumerate(targets):
            store = pltpu.make_async_copy(
                results.at[order, pl.ds(rank * LANES, LANES)], target, out_sem.at[order, rank]
            )
            store.start()
            stores.append(store)
    for store in stores:
        store.wait()


def fill_kernel(filled_ref, first_ref, second_ref, out_ref, sem):
    core = 1 - lax.axis_index("core")
    copies = []
    for which, (quarters, from_them_ref) in enumerate(zip(HALVES, (first_ref, second_ref))):
        for order, (index, _) in enumerate(quarters):
            copies.append(
                pltpu.make_async_copy(
                    from_them_ref.at[:, pl.ds(order * QUARTER, QUARTER)],
                    out_ref.at[:, pl.ds(place_of(core, index), QUARTER)],
                    sem.at[which, order],
                )
            )
    for copy in copies:
        copy.start()
    for copy in copies:
        copy.wait()


HALVES = (((0, 1), (2, 2)), ((1, 1), (3, 1)))


def projected_quarters(quarters, columns, own, blocks, filled):
    last = [] if filled is None else [filled]
    return call(
        functools.partial(project_kernel, quarters),
        (
            jax.ShapeDtypeStruct((LANES, 2 * HALF), jnp.bfloat16),
            jax.ShapeDtypeStruct((LANES, HALF // 2), jnp.bfloat16),
        ),
        [
            pltpu.VMEM((2, ROWS, QUARTER), jnp.bfloat16),
            pltpu.VMEM((2, 2 * LANES, QUARTER), jnp.bfloat16),
            pltpu.SemaphoreType.DMA((2,)),
            pltpu.SemaphoreType.DMA((2, 2)),
        ],
        limit=LAST,
        in_specs=[INSIDE] * 2 + [ANYWHERE] + [INSIDE] * len(blocks) + [ANYWHERE] * len(last),
        out_specs=(ANYWHERE, ANYWHERE),
        input_output_aliases={3 + len(blocks): 0} if last else {},
    )(*columns, own, *blocks, *last)


def swapped(array):
    return moved(array, lambda y, x, z, c: (y, x, z, 1 - c))


def body(signal, gate, filter_taps, skip_weight, out_weight):
    parts = first_quarter(out_weight)
    tables = transform_tables()
    packed, packed_token = call(
        pack_kernel,
        (jax.ShapeDtypeStruct((SEQ_DEVICES * 32, LANES), jnp.bfloat16), TOKEN),
        [pltpu.VMEM((SEQ_DEVICES * 32, LANES), jnp.float32)],
        work=PACK_WORK,
        in_specs=[INSIDE] * 2,
        out_specs=(INSIDE, ANYWHERE),
    )(signal, filter_taps)
    blocks = other_quarters(parts, packed_token)
    arrived = lax.all_to_all(
        packed.reshape(SEQ_DEVICES, 32, LANES), AXES, split_axis=0, concat_axis=0, tiled=True
    )
    convolved = call(
        convolve_kernel,
        jax.ShapeDtypeStruct((SEQ_DEVICES * 16, LANES), jnp.bfloat16),
        [
            pltpu.VMEM((SEQ_DEVICES * 32, LANES), jnp.float32),
            pltpu.VMEM((SEQ_DEVICES * 16, LANES), jnp.float32),
        ],
        limit=CONVOLVE,
        work=WORK,
    )(arrived.reshape(SEQ_DEVICES * 32, LANES), *tables)
    returned = lax.all_to_all(
        convolved.reshape(SEQ_DEVICES, 16, LANES), AXES, split_axis=0, concat_axis=0, tiled=True
    )
    channels, shard_len = signal.shape
    mixed, rounded = call(
        mix_kernel,
        (
            jax.ShapeDtypeStruct((channels, shard_len), jnp.float32),
            jax.ShapeDtypeStruct((PIECES, channels, LANES), jnp.bfloat16),
        ),
        [pltpu.VMEM((SEQ_DEVICES * 16, LANES), jnp.float32)],
        limit=MIX,
        work=WORK,
    )(returned.reshape(SEQ_DEVICES * 16, LANES), signal, gate, skip_weight[:, None])
    mine = lax.all_to_all(rounded, "chan", split_axis=0, concat_axis=0, tiled=True)
    mine = mine.reshape(4 * channels, LANES)
    columns = (mine, swapped(mine))
    lower, across, upper = blocks[1], blocks[2:4], blocks[4]
    filled, first = projected_quarters(HALVES[0], columns, out_weight, [blocks[0], *across], None)
    filled, second = projected_quarters(HALVES[1], columns, out_weight, [lower, upper], filled)
    projected = call(
        fill_kernel,
        jax.ShapeDtypeStruct(filled.shape, filled.dtype),
        [pltpu.SemaphoreType.DMA((2, 2))],
        limit=2,
        in_specs=[ANYWHERE] * 3,
        out_specs=ANYWHERE,
        input_output_aliases={0: 0},
    )(filled, swapped(first), swapped(second))
    return mixed, projected


def solution(mesh):
    fine = Mesh(mesh.devices.reshape(4, 4, 2, 2, 4), (*AXES, "chan"))
    slab = P("chan", AXES)
    in_specs = (slab, slab, slab, P("chan"), P("chan", None))
    out_specs = (slab, P((*AXES, "chan"), None))
    return jax.shard_map(body, mesh=fine, in_specs=in_specs, out_specs=out_specs, check_vma=False)
```

```python
import functools
import itertools

import jax
import jax.numpy as jnp
import ml_dtypes
import numpy as np
from jax import lax
from jax.experimental import pallas as pl
from jax.experimental.pallas import tpu as pltpu
from jax.sharding import Mesh
from jax.sharding import PartitionSpec as P

AXES = ("y", "x", "zh", "core")
SEQ_DEVICES = 64
ROWS = 256
LANES = 128
POSITIONS = ROWS * LANES
OWN_CHANNELS = 4
PIECES = 4
HALF = 4096
QUARTER = 1024
SPLIT = 384
CONVOLVE = 60
MIX = 24
LAST = 48
WORK = 10**11
PACK_WORK = 10**10
JOIN_WORK = 10**10


def transform_tables():
    n1 = (np.arange(SEQ_DEVICES)[None, :] * PIECES + np.arange(PIECES)[:, None]).reshape(-1)
    k1 = np.arange(ROWS) + 0.25
    first = np.exp(-2j * np.pi * np.outer(k1, n1) / ROWS)
    n2 = np.arange(LANES)
    turn = np.exp(-2j * np.pi * np.outer(k1, n2) / POSITIONS)
    second = np.exp(-2j * np.pi * np.outer(n2, n2) / LANES)
    forward_one = np.concatenate([first.real, first.imag], 0)
    forward_two = np.block([[second.real, second.imag], [-second.imag, second.real]])
    back_two = np.block([[second.real, -second.imag], [second.imag, second.real]])
    back_one = np.concatenate([first.real.T, first.imag.T], 1)

    def narrow(table):
        return table.astype(np.float32).astype(ml_dtypes.bfloat16)

    left, right = np.split(back_one, 2, axis=1)
    factors = np.concatenate([forward_one, forward_two, back_two, left, right], 0)
    return narrow(factors), np.concatenate([turn.real, turn.imag], 0).astype(np.float32)


def pack_kernel(signal_ref, filter_ref, out_ref, token_ref, wide):
    for which, source in enumerate((signal_ref, filter_ref)):
        for own in range(OWN_CHANNELS):
            for piece in range(PIECES):
                row = which * 16 + own * PIECES + piece
                wide[pl.ds(row, SEQ_DEVICES, stride=32), :] = source[
                    own * SEQ_DEVICES : (own + 1) * SEQ_DEVICES,
                    piece * LANES : (piece + 1) * LANES,
                ]
    out_ref[...] = wide[...].astype(jnp.bfloat16)


def matmul(left, right):
    return jnp.dot(left, right, preferred_element_type=jnp.float32)


def convolve_kernel(data_ref, factors_ref, turn_ref, out_ref, wide, result):
    forward_one = factors_ref[: 2 * ROWS]
    forward_two, back_two, back_left, back_right = (
        factors_ref[row * ROWS : (row + 1) * ROWS] for row in range(2, 6)
    )
    wide[...] = data_ref[...].astype(jnp.float32)
    columns = []
    for which in range(2):
        for own in range(OWN_CHANNELS):
            pieces = [
                wide[pl.ds(which * 16 + own * PIECES + piece, SEQ_DEVICES, stride=32), :]
                for piece in range(PIECES)
            ]
            columns.append(jnp.concatenate(pieces, axis=0).astype(jnp.bfloat16))
    turn_cos, turn_sin = turn_ref[:ROWS], turn_ref[ROWS:]

    def spectrum(column):
        part = matmul(forward_one, column)
        real, imag = part[:ROWS], part[ROWS:]
        turned = jnp.concatenate(
            [real * turn_cos - imag * turn_sin, real * turn_sin + imag * turn_cos], axis=1
        )
        both = matmul(turned.astype(jnp.bfloat16), forward_two)
        return both[:, :LANES], both[:, LANES:]

    for own in range(OWN_CHANNELS):
        signal_real, signal_imag = spectrum(columns[own])
        filter_real, filter_imag = spectrum(columns[OWN_CHANNELS + own])
        product = jnp.concatenate(
            [
                signal_real * filter_real - signal_imag * filter_imag,
                signal_real * filter_imag + signal_imag * filter_real,
            ],
            axis=1,
        )
        back = matmul(product.astype(jnp.bfloat16), back_two)
        real, imag = back[:, :LANES], back[:, LANES:]
        turned_real = (real * turn_cos + imag * turn_sin).astype(jnp.bfloat16)
        turned_imag = (imag * turn_cos - real * turn_sin).astype(jnp.bfloat16)
        values = matmul(back_left, turned_real) + matmul(back_right, turned_imag)
        values = values * (1.0 / POSITIONS)
        for piece in range(PIECES):
            result[pl.ds(own * PIECES + piece, SEQ_DEVICES, stride=16), :] = values[
                piece * SEQ_DEVICES : (piece + 1) * SEQ_DEVICES
            ]
    out_ref[...] = result[...].astype(jnp.bfloat16)


def mix_kernel(conv_ref, signal_ref, gate_ref, skip_ref, mixed_ref, rounded_ref, wide):
    wide[...] = conv_ref[...].astype(jnp.float32)
    for own in range(OWN_CHANNELS):
        rows = slice(own * SEQ_DEVICES, (own + 1) * SEQ_DEVICES)
        skip = skip_ref[rows, :]
        for piece in range(PIECES):
            lanes = slice(piece * LANES, (piece + 1) * LANES)
            conv = wide[pl.ds(own * PIECES + piece, SEQ_DEVICES, stride=16), :]
            mixed = gate_ref[rows, lanes] * (conv + skip * signal_ref[rows, lanes])
            mixed_ref[rows, lanes] = mixed
            rounded_ref[piece, rows, :] = mixed.astype(jnp.bfloat16)


def call(kernel, out_shape, scratch, limit=60, work=0, **options):
    return pl.pallas_call(
        kernel,
        out_shape=out_shape,
        scratch_shapes=scratch,
        compiler_params=pltpu.CompilerParams(vmem_limit_bytes=limit << 20),
        cost_estimate=pl.CostEstimate(flops=work, bytes_accessed=0, transcendentals=0),
        **options,
    )


def device_pairs(move):
    pairs = []
    for y, x, z, core in itertools.product(range(4), range(4), range(8), range(2)):
        spots = []
        for sy, sx, sz, sc in ((y, x, z, core), move(y, x, z, core)):
            sy, sx, sz = sy % 4, sx % 4, sz % 8
            spots.append((((sy * 4 + sx) * 2 + sz // 4) * 2 + sc) * 4 + sz % 4)
        pairs.append(tuple(spots))
    return pairs


def moved(array, move):
    return lax.ppermute(array, (*AXES, "chan"), device_pairs(move))


def colour(core):
    x, y = lax.axis_index("x"), lax.axis_index("y")
    return jnp.where(core == 0, x + 2 * y, 2 * x + y) % 4


def join_kernel(below_ref, above_ref, far_ref, after_ref, out_ref, sem):
    copies = [
        pltpu.make_async_copy(ref, out_ref.at[pl.ds(index * ROWS, ROWS)], sem.at[index])
        for index, ref in enumerate((below_ref, above_ref, far_ref))
    ]
    for copy in copies:
        copy.start()
    for copy in copies:
        copy.wait()


ANYWHERE = pl.BlockSpec(memory_space=pl.ANY)
INSIDE = pl.BlockSpec(memory_space=pltpu.VMEM)
TOKEN = jax.ShapeDtypeStruct((8, LANES), jnp.float32)


def first_quarter(out_weight):
    core = lax.axis_index("core")
    start = core * HALF + colour(core) * QUARTER
    mine = lax.dynamic_slice_in_dim(out_weight, start, QUARTER, 1)
    below = moved(mine, lambda y, x, z, c: (y, x, z + 1, c))
    above = moved(mine, lambda y, x, z, c: (y, x, z - 1, c))
    far = moved(mine, lambda y, x, z, c: (y, x, z + 2 - 4 * c, c))
    return below, above, far


def other_quarters(parts, after):
    block = call(
        join_kernel,
        jax.ShapeDtypeStruct((3 * ROWS, QUARTER), jnp.bfloat16),
        [pltpu.SemaphoreType.DMA((3,))],
        limit=2,
        work=JOIN_WORK,
        in_specs=[ANYWHERE] * 4,
        out_specs=ANYWHERE,
    )(*parts, after)
    upper, lower = block[:SPLIT], block[SPLIT:]
    return [
        block,
        moved(block, lambda y, x, z, c: (y - c, x - 1 + c, z, c)),
        moved(upper, lambda y, x, z, c: (y + 1 - c, x + c, z, c)),
        moved(lower, lambda y, x, z, c: (y - 1 + c, x - c, z, c)),
        moved(block, lambda y, x, z, c: (y + c, x + 1 - c, z, c)),
    ]


def place_of(core, index):
    return pl.multiple_of(core * HALF + (colour(core) + index) % 4 * QUARTER, QUARTER)


def transposed_columns(mine_ref, theirs_ref):
    chan = lax.axis_index("chan")
    rows = [
        jnp.concatenate(
            [
                ref[pl.ds(pl.multiple_of((chan + shift) % 4 * ROWS, ROWS), ROWS), :].T
                for ref in (mine_ref, theirs_ref)
            ],
            axis=0,
        )
        for shift in (0, 3, 1, 2)
    ]
    return jnp.concatenate(rows, axis=1)


def project_kernel(quarters, given, *refs):
    count = sum(parts for _, parts in quarters)
    columns_refs, own_ref = refs[:given], refs[given]
    block_refs = refs[given + 1 : given + 1 + count]
    weights, results, load_sem, out_sem = refs[-4:]
    out_ref, for_them_ref = refs[-6:-4] if given == 1 else refs[-7:-5]
    core = lax.axis_index("core")
    loads, part = [], 0
    for order, (index, parts) in enumerate(quarters):
        sources = [own_ref.at[:, pl.ds(place_of(core, index), QUARTER)]]
        sources += block_refs[part : part + parts]
        part += parts
        group, row = [], 0
        for which, source in enumerate(sources):
            depth = ROWS if which == 0 else source.shape[0]
            group.append(
                pltpu.make_async_copy(
                    source, weights.at[order, pl.ds(row, depth)], load_sem.at[order, which]
                )
            )
            row += depth
        for load in group:
            load.start()
        loads.append(group)
    if given == 1:
        columns = columns_refs[0][...]
    else:
        columns = transposed_columns(*columns_refs)
        refs[-5][...] = columns
    stores = []
    for order, (index, _) in enumerate(quarters):
        for load in loads[order]:
            load.wait()
        results[order] = matmul(columns, weights[order]).astype(jnp.bfloat16)
        targets = (
            out_ref.at[:, pl.ds(place_of(core, index), QUARTER)],
            for_them_ref.at[:, pl.ds(order * QUARTER, QUARTER)],
        )
        for rank, target in enumerate(targets):
            store = pltpu.make_async_copy(
                results.at[order, pl.ds(rank * LANES, LANES)], target, out_sem.at[order, rank]
            )
            store.start()
            stores.append(store)
    for store in stores:
        store.wait()


def fill_kernel(filled_ref, first_ref, second_ref, out_ref, sem):
    core = 1 - lax.axis_index("core")
    copies = []
    for which, (quarters, from_them_ref) in enumerate(zip(HALVES, (first_ref, second_ref))):
        for order, (index, _) in enumerate(quarters):
            copies.append(
                pltpu.make_async_copy(
                    from_them_ref.at[:, pl.ds(order * QUARTER, QUARTER)],
                    out_ref.at[:, pl.ds(place_of(core, index), QUARTER)],
                    sem.at[which, order],
                )
            )
    for copy in copies:
        copy.start()
    for copy in copies:
        copy.wait()


HALVES = (((0, 1), (2, 2)), ((1, 1), (3, 1)))


def projected_quarters(quarters, columns, own, blocks, filled):
    last = [] if filled is None else [filled]
    shapes = [
        jax.ShapeDtypeStruct((LANES, 2 * HALF), jnp.bfloat16),
        jax.ShapeDtypeStruct((LANES, HALF // 2), jnp.bfloat16),
    ]
    places = [ANYWHERE, ANYWHERE]
    if not last:
        shapes.append(jax.ShapeDtypeStruct((2 * LANES, 4 * ROWS), jnp.bfloat16))
        places.append(INSIDE)
    return call(
        functools.partial(project_kernel, quarters, len(columns)),
        tuple(shapes),
        [
            pltpu.VMEM((2, 4 * ROWS, QUARTER), jnp.bfloat16),
            pltpu.VMEM((2, 2 * LANES, QUARTER), jnp.bfloat16),
            pltpu.SemaphoreType.DMA((2, 3)),
            pltpu.SemaphoreType.DMA((2, 2)),
        ],
        limit=LAST,
        in_specs=[INSIDE] * len(columns) + [ANYWHERE] * (1 + len(blocks) + len(last)),
        out_specs=tuple(places),
        input_output_aliases={len(columns) + 1 + len(blocks): 0} if last else {},
    )(*columns, own, *blocks, *last)


def swapped(array):
    return moved(array, lambda y, x, z, c: (y, x, z, 1 - c))


def body(signal, gate, filter_taps, skip_weight, out_weight):
    parts = first_quarter(out_weight)
    tables = transform_tables()
    packed, packed_token = call(
        pack_kernel,
        (jax.ShapeDtypeStruct((SEQ_DEVICES * 32, LANES), jnp.bfloat16), TOKEN),
        [pltpu.VMEM((SEQ_DEVICES * 32, LANES), jnp.float32)],
        work=PACK_WORK,
        in_specs=[INSIDE] * 2,
        out_specs=(INSIDE, ANYWHERE),
    )(signal, filter_taps)
    blocks = other_quarters(parts, packed_token)
    arrived = lax.all_to_all(
        packed.reshape(SEQ_DEVICES, 32, LANES), AXES, split_axis=0, concat_axis=0, tiled=True
    )
    convolved = call(
        convolve_kernel,
        jax.ShapeDtypeStruct((SEQ_DEVICES * 16, LANES), jnp.bfloat16),
        [
            pltpu.VMEM((SEQ_DEVICES * 32, LANES), jnp.float32),
            pltpu.VMEM((SEQ_DEVICES * 16, LANES), jnp.float32),
        ],
        limit=CONVOLVE,
        work=WORK,
    )(arrived.reshape(SEQ_DEVICES * 32, LANES), *tables)
    returned = lax.all_to_all(
        convolved.reshape(SEQ_DEVICES, 16, LANES), AXES, split_axis=0, concat_axis=0, tiled=True
    )
    channels, shard_len = signal.shape
    mixed, rounded = call(
        mix_kernel,
        (
            jax.ShapeDtypeStruct((channels, shard_len), jnp.float32),
            jax.ShapeDtypeStruct((PIECES, channels, LANES), jnp.bfloat16),
        ),
        [pltpu.VMEM((SEQ_DEVICES * 16, LANES), jnp.float32)],
        limit=MIX,
        work=WORK,
    )(returned.reshape(SEQ_DEVICES * 16, LANES), signal, gate, skip_weight[:, None])
    mine = lax.all_to_all(rounded, "chan", split_axis=0, concat_axis=0, tiled=True)
    mine = mine.reshape(4 * channels, LANES)
    columns = (mine, swapped(mine))
    lower, across, upper = blocks[1], blocks[2:4], blocks[4]
    filled, first, turned = projected_quarters(
        HALVES[0], columns, out_weight, [blocks[0], *across], None
    )
    filled, second = projected_quarters(
        HALVES[1], [turned], out_weight, [lower, upper], filled
    )
    projected = call(
        fill_kernel,
        jax.ShapeDtypeStruct(filled.shape, filled.dtype),
        [pltpu.SemaphoreType.DMA((2, 2))],
        limit=2,
        in_specs=[ANYWHERE] * 3,
        out_specs=ANYWHERE,
        input_output_aliases={0: 0},
    )(filled, swapped(first), swapped(second))
    return mixed, projected


def solution(mesh):
    fine = Mesh(mesh.devices.reshape(4, 4, 2, 2, 4), (*AXES, "chan"))
    slab = P("chan", AXES)
    in_specs = (slab, slab, slab, P("chan"), P("chan", None))
    out_specs = (slab, P((*AXES, "chan"), None))
    return jax.shard_map(body, mesh=fine, in_specs=in_specs, out_specs=out_specs, check_vma=False)
```

```python
import functools
import itertools

import jax
import jax.numpy as jnp
import ml_dtypes
import numpy as np
from jax import lax
from jax.experimental import pallas as pl
from jax.experimental.pallas import tpu as pltpu
from jax.sharding import Mesh
from jax.sharding import PartitionSpec as P

AXES = ("y", "x", "zh", "core")
SEQ_DEVICES = 64
ROWS = 256
LANES = 128
POSITIONS = ROWS * LANES
OWN_CHANNELS = 4
PIECES = 4
HALF = 4096
QUARTER = 1024
SPLIT = 384
CONVOLVE = 60
MIX = 24
LAST = 48
WORK = 10**11
PACK_WORK = 10**10
JOIN_WORK = 10**10


def transform_tables():
    n1 = (np.arange(SEQ_DEVICES)[None, :] * PIECES + np.arange(PIECES)[:, None]).reshape(-1)
    k1 = np.arange(ROWS) + 0.25
    first = np.exp(-2j * np.pi * np.outer(k1, n1) / ROWS)
    n2 = np.arange(LANES)
    turn = np.exp(-2j * np.pi * np.outer(k1, n2) / POSITIONS)
    second = np.exp(-2j * np.pi * np.outer(n2, n2) / LANES)
    forward_one = np.concatenate([first.real, first.imag], 0)
    forward_two = np.block([[second.real, second.imag], [-second.imag, second.real]])
    back_two = np.block([[second.real, -second.imag], [second.imag, second.real]])
    back_one = np.concatenate([first.real.T, first.imag.T], 1)

    def narrow(table):
        return table.astype(np.float32).astype(ml_dtypes.bfloat16)

    left, right = np.split(back_one, 2, axis=1)
    factors = np.concatenate([forward_one, forward_two, back_two, left, right], 0)
    return narrow(factors), np.concatenate([turn.real, turn.imag], 0).astype(np.float32)


def pack_kernel(signal_ref, filter_ref, out_ref, token_ref, wide):
    for which, source in enumerate((signal_ref, filter_ref)):
        for own in range(OWN_CHANNELS):
            for piece in range(PIECES):
                row = which * 16 + own * PIECES + piece
                wide[pl.ds(row, SEQ_DEVICES, stride=32), :] = source[
                    own * SEQ_DEVICES : (own + 1) * SEQ_DEVICES,
                    piece * LANES : (piece + 1) * LANES,
                ]
    out_ref[...] = wide[...].astype(jnp.bfloat16)


def matmul(left, right):
    return jnp.dot(left, right, preferred_element_type=jnp.float32)


def convolve_kernel(data_ref, factors_ref, turn_ref, out_ref, wide, result):
    forward_one = factors_ref[: 2 * ROWS]
    forward_two, back_two, back_left, back_right = (
        factors_ref[row * ROWS : (row + 1) * ROWS] for row in range(2, 6)
    )
    wide[...] = data_ref[...].astype(jnp.float32)
    columns = []
    for which in range(2):
        for own in range(OWN_CHANNELS):
            pieces = [
                wide[pl.ds(which * 16 + own * PIECES + piece, SEQ_DEVICES, stride=32), :]
                for piece in range(PIECES)
            ]
            columns.append(jnp.concatenate(pieces, axis=0).astype(jnp.bfloat16))
    turn_cos, turn_sin = turn_ref[:ROWS], turn_ref[ROWS:]

    def spectrum(column):
        part = matmul(forward_one, column)
        real, imag = part[:ROWS], part[ROWS:]
        turned = jnp.concatenate(
            [real * turn_cos - imag * turn_sin, real * turn_sin + imag * turn_cos], axis=1
        )
        both = matmul(turned.astype(jnp.bfloat16), forward_two)
        return both[:, :LANES], both[:, LANES:]

    for own in range(OWN_CHANNELS):
        signal_real, signal_imag = spectrum(columns[own])
        filter_real, filter_imag = spectrum(columns[OWN_CHANNELS + own])
        product = jnp.concatenate(
            [
                signal_real * filter_real - signal_imag * filter_imag,
                signal_real * filter_imag + signal_imag * filter_real,
            ],
            axis=1,
        )
        back = matmul(product.astype(jnp.bfloat16), back_two)
        real, imag = back[:, :LANES], back[:, LANES:]
        turned_real = (real * turn_cos + imag * turn_sin).astype(jnp.bfloat16)
        turned_imag = (imag * turn_cos - real * turn_sin).astype(jnp.bfloat16)
        values = matmul(back_left, turned_real) + matmul(back_right, turned_imag)
        values = values * (1.0 / POSITIONS)
        for piece in range(PIECES):
            result[pl.ds(own * PIECES + piece, SEQ_DEVICES, stride=16), :] = values[
                piece * SEQ_DEVICES : (piece + 1) * SEQ_DEVICES
            ]
    out_ref[...] = result[...].astype(jnp.bfloat16)


def mix_kernel(conv_ref, signal_ref, gate_ref, skip_ref, mixed_ref, rounded_ref, wide):
    wide[...] = conv_ref[...].astype(jnp.float32)
    for own in range(OWN_CHANNELS):
        rows = slice(own * SEQ_DEVICES, (own + 1) * SEQ_DEVICES)
        skip = skip_ref[rows, :]
        for piece in range(PIECES):
            lanes = slice(piece * LANES, (piece + 1) * LANES)
            conv = wide[pl.ds(own * PIECES + piece, SEQ_DEVICES, stride=16), :]
            mixed = gate_ref[rows, lanes] * (conv + skip * signal_ref[rows, lanes])
            mixed_ref[rows, lanes] = mixed
            rounded_ref[piece, rows, :] = mixed.astype(jnp.bfloat16)


def call(kernel, out_shape, scratch, limit=60, work=0, **options):
    return pl.pallas_call(
        kernel,
        out_shape=out_shape,
        scratch_shapes=scratch,
        compiler_params=pltpu.CompilerParams(vmem_limit_bytes=limit << 20),
        cost_estimate=pl.CostEstimate(flops=work, bytes_accessed=0, transcendentals=0),
        **options,
    )


def device_pairs(move):
    pairs = []
    for y, x, z, core in itertools.product(range(4), range(4), range(8), range(2)):
        spots = []
        for sy, sx, sz, sc in ((y, x, z, core), move(y, x, z, core)):
            sy, sx, sz = sy % 4, sx % 4, sz % 8
            spots.append((((sy * 4 + sx) * 2 + sz // 4) * 2 + sc) * 4 + sz % 4)
        pairs.append(tuple(spots))
    return pairs


def moved(array, move):
    return lax.ppermute(array, (*AXES, "chan"), device_pairs(move))


def colour(core):
    x, y = lax.axis_index("x"), lax.axis_index("y")
    return jnp.where(core == 0, x + 2 * y, 2 * x + y) % 4


def join_kernel(below_ref, above_ref, far_ref, after_ref, out_ref, sem):
    copies = [
        pltpu.make_async_copy(ref, out_ref.at[pl.ds(index * ROWS, ROWS)], sem.at[index])
        for index, ref in enumerate((below_ref, above_ref, far_ref))
    ]
    for copy in copies:
        copy.start()
    for copy in copies:
        copy.wait()


ANYWHERE = pl.BlockSpec(memory_space=pl.ANY)
INSIDE = pl.BlockSpec(memory_space=pltpu.VMEM)
TOKEN = jax.ShapeDtypeStruct((8, LANES), jnp.float32)


def first_quarter(out_weight):
    core = lax.axis_index("core")
    start = core * HALF + colour(core) * QUARTER
    mine = lax.dynamic_slice_in_dim(out_weight, start, QUARTER, 1)
    below = moved(mine, lambda y, x, z, c: (y, x, z + 1, c))
    above = moved(mine, lambda y, x, z, c: (y, x, z - 1, c))
    far = moved(above, lambda y, x, z, c: (y, x, z - 1, c))
    return below, above, far


def other_quarters(parts, after):
    block = call(
        join_kernel,
        jax.ShapeDtypeStruct((3 * ROWS, QUARTER), jnp.bfloat16),
        [pltpu.SemaphoreType.DMA((3,))],
        limit=2,
        work=JOIN_WORK,
        in_specs=[ANYWHERE] * 4,
        out_specs=ANYWHERE,
    )(*parts, after)
    upper, lower = block[:SPLIT], block[SPLIT:]
    return [
        block,
        moved(block, lambda y, x, z, c: (y - c, x - 1 + c, z, c)),
        moved(upper, lambda y, x, z, c: (y + 1 - c, x + c, z, c)),
        moved(lower, lambda y, x, z, c: (y - 1 + c, x - c, z, c)),
        moved(block, lambda y, x, z, c: (y + c, x + 1 - c, z, c)),
    ]


def place_of(core, index):
    return pl.multiple_of(core * HALF + (colour(core) + index) % 4 * QUARTER, QUARTER)


def transposed_columns(mine_ref, theirs_ref):
    chan = lax.axis_index("chan")
    rows = [
        jnp.concatenate(
            [
                ref[pl.ds(pl.multiple_of((chan + shift) % 4 * ROWS, ROWS), ROWS), :].T
                for ref in (mine_ref, theirs_ref)
            ],
            axis=0,
        )
        for shift in (0, 3, 1, 2)
    ]
    return jnp.concatenate(rows, axis=1)


def project_kernel(quarters, given, *refs):
    count = sum(parts for _, parts in quarters)
    columns_refs, own_ref = refs[:given], refs[given]
    block_refs = refs[given + 1 : given + 1 + count]
    weights, results, load_sem, out_sem = refs[-4:]
    out_ref, for_them_ref = refs[-6:-4] if given == 1 else refs[-7:-5]
    core = lax.axis_index("core")
    loads, part = [], 0
    for order, (index, parts) in enumerate(quarters):
        sources = [own_ref.at[:, pl.ds(place_of(core, index), QUARTER)]]
        sources += block_refs[part : part + parts]
        part += parts
        group, row = [], 0
        for which, source in enumerate(sources):
            depth = ROWS if which == 0 else source.shape[0]
            group.append(
                pltpu.make_async_copy(
                    source, weights.at[order, pl.ds(row, depth)], load_sem.at[order, which]
                )
            )
            row += depth
        for load in group:
            load.start()
        loads.append(group)
    if given == 1:
        columns = columns_refs[0][...]
    else:
        columns = transposed_columns(*columns_refs)
        refs[-5][...] = columns
    stores = []
    for order, (index, _) in enumerate(quarters):
        for load in loads[order]:
            load.wait()
        results[order] = matmul(columns, weights[order]).astype(jnp.bfloat16)
        targets = (
            out_ref.at[:, pl.ds(place_of(core, index), QUARTER)],
            for_them_ref.at[:, pl.ds(order * QUARTER, QUARTER)],
        )
        for rank, target in enumerate(targets):
            store = pltpu.make_async_copy(
                results.at[order, pl.ds(rank * LANES, LANES)], target, out_sem.at[order, rank]
            )
            store.start()
            stores.append(store)
    for store in stores:
        store.wait()


def fill_kernel(filled_ref, first_ref, second_ref, out_ref, sem):
    core = 1 - lax.axis_index("core")
    copies = []
    for which, (quarters, from_them_ref) in enumerate(zip(HALVES, (first_ref, second_ref))):
        for order, (index, _) in enumerate(quarters):
            copies.append(
                pltpu.make_async_copy(
                    from_them_ref.at[:, pl.ds(order * QUARTER, QUARTER)],
                    out_ref.at[:, pl.ds(place_of(core, index), QUARTER)],
                    sem.at[which, order],
                )
            )
    for copy in copies:
        copy.start()
    for copy in copies:
        copy.wait()


HALVES = (((0, 1), (2, 2)), ((1, 1), (3, 1)))


def projected_quarters(quarters, columns, own, blocks, filled):
    last = [] if filled is None else [filled]
    shapes = [
        jax.ShapeDtypeStruct((LANES, 2 * HALF), jnp.bfloat16),
        jax.ShapeDtypeStruct((LANES, HALF // 2), jnp.bfloat16),
    ]
    places = [ANYWHERE, ANYWHERE]
    if not last:
        shapes.append(jax.ShapeDtypeStruct((2 * LANES, 4 * ROWS), jnp.bfloat16))
        places.append(INSIDE)
    return call(
        functools.partial(project_kernel, quarters, len(columns)),
        tuple(shapes),
        [
            pltpu.VMEM((2, 4 * ROWS, QUARTER), jnp.bfloat16),
            pltpu.VMEM((2, 2 * LANES, QUARTER), jnp.bfloat16),
            pltpu.SemaphoreType.DMA((2, 3)),
            pltpu.SemaphoreType.DMA((2, 2)),
        ],
        limit=LAST,
        in_specs=[INSIDE] * len(columns) + [ANYWHERE] * (1 + len(blocks) + len(last)),
        out_specs=tuple(places),
        input_output_aliases={len(columns) + 1 + len(blocks): 0} if last else {},
    )(*columns, own, *blocks, *last)


def swapped(array):
    return moved(array, lambda y, x, z, c: (y, x, z, 1 - c))


def body(signal, gate, filter_taps, skip_weight, out_weight):
    parts = first_quarter(out_weight)
    tables = transform_tables()
    packed, packed_token = call(
        pack_kernel,
        (jax.ShapeDtypeStruct((SEQ_DEVICES * 32, LANES), jnp.bfloat16), TOKEN),
        [pltpu.VMEM((SEQ_DEVICES * 32, LANES), jnp.float32)],
        work=PACK_WORK,
        in_specs=[INSIDE] * 2,
        out_specs=(INSIDE, ANYWHERE),
    )(signal, filter_taps)
    blocks = other_quarters(parts, packed_token)
    arrived = lax.all_to_all(
        packed.reshape(SEQ_DEVICES, 32, LANES), AXES, split_axis=0, concat_axis=0, tiled=True
    )
    convolved = call(
        convolve_kernel,
        jax.ShapeDtypeStruct((SEQ_DEVICES * 16, LANES), jnp.bfloat16),
        [
            pltpu.VMEM((SEQ_DEVICES * 32, LANES), jnp.float32),
            pltpu.VMEM((SEQ_DEVICES * 16, LANES), jnp.float32),
        ],
        limit=CONVOLVE,
        work=WORK,
    )(arrived.reshape(SEQ_DEVICES * 32, LANES), *tables)
    returned = lax.all_to_all(
        convolved.reshape(SEQ_DEVICES, 16, LANES), AXES, split_axis=0, concat_axis=0, tiled=True
    )
    channels, shard_len = signal.shape
    mixed, rounded = call(
        mix_kernel,
        (
            jax.ShapeDtypeStruct((channels, shard_len), jnp.float32),
            jax.ShapeDtypeStruct((PIECES, channels, LANES), jnp.bfloat16),
        ),
        [pltpu.VMEM((SEQ_DEVICES * 16, LANES), jnp.float32)],
        limit=MIX,
        work=WORK,
    )(returned.reshape(SEQ_DEVICES * 16, LANES), signal, gate, skip_weight[:, None])
    mine = lax.all_to_all(rounded, "chan", split_axis=0, concat_axis=0, tiled=True)
    mine = mine.reshape(4 * channels, LANES)
    columns = (mine, swapped(mine))
    lower, across, upper = blocks[1], blocks[2:4], blocks[4]
    filled, first, turned = projected_quarters(
        HALVES[0], columns, out_weight, [blocks[0], *across], None
    )
    filled, second = projected_quarters(
        HALVES[1], [turned], out_weight, [lower, upper], filled
    )
    projected = call(
        fill_kernel,
        jax.ShapeDtypeStruct(filled.shape, filled.dtype),
        [pltpu.SemaphoreType.DMA((2, 2))],
        limit=2,
        in_specs=[ANYWHERE] * 3,
        out_specs=ANYWHERE,
        input_output_aliases={0: 0},
    )(filled, swapped(first), swapped(second))
    return mixed, projected


def solution(mesh):
    fine = Mesh(mesh.devices.reshape(4, 4, 2, 2, 4), (*AXES, "chan"))
    slab = P("chan", AXES)
    in_specs = (slab, slab, slab, P("chan"), P("chan", None))
    out_specs = (slab, P((*AXES, "chan"), None))
    return jax.shard_map(body, mesh=fine, in_specs=in_specs, out_specs=out_specs, check_vma=False)
```

```python
import functools
import itertools

import jax
import jax.numpy as jnp
import ml_dtypes
import numpy as np
from jax import lax
from jax.experimental import pallas as pl
from jax.experimental.pallas import tpu as pltpu
from jax.sharding import Mesh
from jax.sharding import PartitionSpec as P

AXES = ("y", "x", "zh", "core")
SEQ_DEVICES = 64
ROWS = 256
LANES = 128
POSITIONS = ROWS * LANES
OWN_CHANNELS = 4
PIECES = 4
HALF = 4096
QUARTER = 1024
SPLIT = 384
CONVOLVE = 60
MIX = 24
LAST = 48
WORK = 10**11
PACK_WORK = 10**10
JOIN_WORK = 10**10


def transform_tables():
    n1 = (np.arange(SEQ_DEVICES)[None, :] * PIECES + np.arange(PIECES)[:, None]).reshape(-1)
    k1 = np.arange(ROWS) + 0.25
    first = np.exp(-2j * np.pi * np.outer(k1, n1) / ROWS)
    n2 = np.arange(LANES)
    turn = np.exp(-2j * np.pi * np.outer(k1, n2) / POSITIONS)
    second = np.exp(-2j * np.pi * np.outer(n2, n2) / LANES)
    forward_one = np.concatenate([first.real, first.imag], 0)
    forward_two = np.block([[second.real, second.imag], [-second.imag, second.real]])
    back_two = np.block([[second.real, -second.imag], [second.imag, second.real]])
    back_one = np.concatenate([first.real.T, first.imag.T], 1)

    def narrow(table):
        return table.astype(np.float32).astype(ml_dtypes.bfloat16)

    left, right = np.split(back_one, 2, axis=1)
    factors = np.concatenate([forward_one, forward_two, back_two, left, right], 0)
    return narrow(factors), np.concatenate([turn.real, turn.imag], 0).astype(np.float32)


def pack_kernel(signal_ref, filter_ref, own_ref, out_ref, token_ref, mine_ref, wide, sem):
    core = lax.axis_index("core")
    slice_copy = pltpu.make_async_copy(own_ref.at[:, pl.ds(place_of(core, 0), QUARTER)], mine_ref, sem)
    slice_copy.start()
    for which, source in enumerate((signal_ref, filter_ref)):
        for own in range(OWN_CHANNELS):
            for piece in range(PIECES):
                row = which * 16 + own * PIECES + piece
                wide[pl.ds(row, SEQ_DEVICES, stride=32), :] = source[
                    own * SEQ_DEVICES : (own + 1) * SEQ_DEVICES,
                    piece * LANES : (piece + 1) * LANES,
                ]
    out_ref[...] = wide[...].astype(jnp.bfloat16)
    slice_copy.wait()


def matmul(left, right):
    return jnp.dot(left, right, preferred_element_type=jnp.float32)


def convolve_kernel(data_ref, factors_ref, turn_ref, out_ref, wide, result):
    forward_one = factors_ref[: 2 * ROWS]
    forward_two, back_two, back_left, back_right = (
        factors_ref[row * ROWS : (row + 1) * ROWS] for row in range(2, 6)
    )
    wide[...] = data_ref[...].astype(jnp.float32)
    columns = []
    for which in range(2):
        for own in range(OWN_CHANNELS):
            pieces = [
                wide[pl.ds(which * 16 + own * PIECES + piece, SEQ_DEVICES, stride=32), :]
                for piece in range(PIECES)
            ]
            columns.append(jnp.concatenate(pieces, axis=0).astype(jnp.bfloat16))
    turn_cos, turn_sin = turn_ref[:ROWS], turn_ref[ROWS:]

    def spectrum(column):
        part = matmul(forward_one, column)
        real, imag = part[:ROWS], part[ROWS:]
        turned = jnp.concatenate(
            [real * turn_cos - imag * turn_sin, real * turn_sin + imag * turn_cos], axis=1
        )
        both = matmul(turned.astype(jnp.bfloat16), forward_two)
        return both[:, :LANES], both[:, LANES:]

    for own in range(OWN_CHANNELS):
        signal_real, signal_imag = spectrum(columns[own])
        filter_real, filter_imag = spectrum(columns[OWN_CHANNELS + own])
        product = jnp.concatenate(
            [
                signal_real * filter_real - signal_imag * filter_imag,
                signal_real * filter_imag + signal_imag * filter_real,
            ],
            axis=1,
        )
        back = matmul(product.astype(jnp.bfloat16), back_two)
        real, imag = back[:, :LANES], back[:, LANES:]
        turned_real = (real * turn_cos + imag * turn_sin).astype(jnp.bfloat16)
        turned_imag = (imag * turn_cos - real * turn_sin).astype(jnp.bfloat16)
        values = matmul(back_left, turned_real) + matmul(back_right, turned_imag)
        values = values * (1.0 / POSITIONS)
        for piece in range(PIECES):
            result[pl.ds(own * PIECES + piece, SEQ_DEVICES, stride=16), :] = values[
                piece * SEQ_DEVICES : (piece + 1) * SEQ_DEVICES
            ]
    out_ref[...] = result[...].astype(jnp.bfloat16)


def mix_kernel(conv_ref, signal_ref, gate_ref, skip_ref, mixed_ref, rounded_ref, wide):
    wide[...] = conv_ref[...].astype(jnp.float32)
    for own in range(OWN_CHANNELS):
        rows = slice(own * SEQ_DEVICES, (own + 1) * SEQ_DEVICES)
        skip = skip_ref[rows, :]
        for piece in range(PIECES):
            lanes = slice(piece * LANES, (piece + 1) * LANES)
            conv = wide[pl.ds(own * PIECES + piece, SEQ_DEVICES, stride=16), :]
            mixed = gate_ref[rows, lanes] * (conv + skip * signal_ref[rows, lanes])
            mixed_ref[rows, lanes] = mixed
            rounded_ref[piece, rows, :] = mixed.astype(jnp.bfloat16)


def call(kernel, out_shape, scratch, limit=60, work=0, **options):
    return pl.pallas_call(
        kernel,
        out_shape=out_shape,
        scratch_shapes=scratch,
        compiler_params=pltpu.CompilerParams(vmem_limit_bytes=limit << 20),
        cost_estimate=pl.CostEstimate(flops=work, bytes_accessed=0, transcendentals=0),
        **options,
    )


def device_pairs(move):
    pairs = []
    for y, x, z, core in itertools.product(range(4), range(4), range(8), range(2)):
        spots = []
        for sy, sx, sz, sc in ((y, x, z, core), move(y, x, z, core)):
            sy, sx, sz = sy % 4, sx % 4, sz % 8
            spots.append((((sy * 4 + sx) * 2 + sz // 4) * 2 + sc) * 4 + sz % 4)
        pairs.append(tuple(spots))
    return pairs


def moved(array, move):
    return lax.ppermute(array, (*AXES, "chan"), device_pairs(move))


def colour(core):
    x, y = lax.axis_index("x"), lax.axis_index("y")
    return jnp.where(core == 0, x + 2 * y, 2 * x + y) % 4


def join_kernel(below_ref, above_ref, far_ref, after_ref, out_ref, sem):
    copies = [
        pltpu.make_async_copy(ref, out_ref.at[pl.ds(index * ROWS, ROWS)], sem.at[index])
        for index, ref in enumerate((below_ref, above_ref, far_ref))
    ]
    for copy in copies:
        copy.start()
    for copy in copies:
        copy.wait()


ANYWHERE = pl.BlockSpec(memory_space=pl.ANY)
INSIDE = pl.BlockSpec(memory_space=pltpu.VMEM)
TOKEN = jax.ShapeDtypeStruct((8, LANES), jnp.float32)


def first_quarter(mine):
    below = moved(mine, lambda y, x, z, c: (y, x, z + 1, c))
    above = moved(mine, lambda y, x, z, c: (y, x, z - 1, c))
    far = moved(mine, lambda y, x, z, c: (y, x, z + 2 - 4 * c, c))
    return below, above, far


def other_quarters(parts, after):
    block = call(
        join_kernel,
        jax.ShapeDtypeStruct((3 * ROWS, QUARTER), jnp.bfloat16),
        [pltpu.SemaphoreType.DMA((3,))],
        limit=2,
        work=JOIN_WORK,
        in_specs=[ANYWHERE] * 4,
        out_specs=ANYWHERE,
    )(*parts, after)
    upper, lower = block[:SPLIT], block[SPLIT:]
    return [
        block,
        moved(block, lambda y, x, z, c: (y - c, x - 1 + c, z, c)),
        moved(upper, lambda y, x, z, c: (y + 1 - c, x + c, z, c)),
        moved(lower, lambda y, x, z, c: (y - 1 + c, x - c, z, c)),
        moved(block, lambda y, x, z, c: (y + c, x + 1 - c, z, c)),
    ]


def place_of(core, index):
    return pl.multiple_of(core * HALF + (colour(core) + index) % 4 * QUARTER, QUARTER)


def transposed_columns(mine_ref, theirs_ref):
    chan = lax.axis_index("chan")
    rows = [
        jnp.concatenate(
            [
                ref[pl.ds(pl.multiple_of((chan + shift) % 4 * ROWS, ROWS), ROWS), :].T
                for ref in (mine_ref, theirs_ref)
            ],
            axis=0,
        )
        for shift in (0, 3, 1, 2)
    ]
    return jnp.concatenate(rows, axis=1)


def project_kernel(quarters, given, *refs):
    count = sum(parts for _, parts in quarters)
    columns_refs, own_ref = refs[:given], refs[given]
    block_refs = refs[given + 1 : given + 1 + count]
    weights, results, load_sem, out_sem = refs[-4:]
    out_ref, for_them_ref = refs[-6:-4] if given == 1 else refs[-7:-5]
    core = lax.axis_index("core")
    loads, part = [], 0
    for order, (index, parts) in enumerate(quarters):
        sources = [own_ref.at[:, pl.ds(place_of(core, index), QUARTER)]]
        sources += block_refs[part : part + parts]
        part += parts
        group, row = [], 0
        for which, source in enumerate(sources):
            depth = ROWS if which == 0 else source.shape[0]
            group.append(
                pltpu.make_async_copy(
                    source, weights.at[order, pl.ds(row, depth)], load_sem.at[order, which]
                )
            )
            row += depth
        for load in group:
            load.start()
        loads.append(group)
    if given == 1:
        columns = columns_refs[0][...]
    else:
        columns = transposed_columns(*columns_refs)
        refs[-5][...] = columns
    stores = []
    for order, (index, _) in enumerate(quarters):
        for load in loads[order]:
            load.wait()
        results[order] = matmul(columns, weights[order]).astype(jnp.bfloat16)
        targets = (
            out_ref.at[:, pl.ds(place_of(core, index), QUARTER)],
            for_them_ref.at[:, pl.ds(order * QUARTER, QUARTER)],
        )
        for rank, target in enumerate(targets):
            store = pltpu.make_async_copy(
                results.at[order, pl.ds(rank * LANES, LANES)], target, out_sem.at[order, rank]
            )
            store.start()
            stores.append(store)
    for store in stores:
        store.wait()


def fill_kernel(filled_ref, first_ref, second_ref, out_ref, sem):
    core = 1 - lax.axis_index("core")
    copies = []
    for which, (quarters, from_them_ref) in enumerate(zip(HALVES, (first_ref, second_ref))):
        for order, (index, _) in enumerate(quarters):
            copies.append(
                pltpu.make_async_copy(
                    from_them_ref.at[:, pl.ds(order * QUARTER, QUARTER)],
                    out_ref.at[:, pl.ds(place_of(core, index), QUARTER)],
                    sem.at[which, order],
                )
            )
    for copy in copies:
        copy.start()
    for copy in copies:
        copy.wait()


HALVES = (((0, 1), (2, 2)), ((1, 1), (3, 1)))


def projected_quarters(quarters, columns, own, blocks, filled):
    last = [] if filled is None else [filled]
    shapes = [
        jax.ShapeDtypeStruct((LANES, 2 * HALF), jnp.bfloat16),
        jax.ShapeDtypeStruct((LANES, HALF // 2), jnp.bfloat16),
    ]
    places = [ANYWHERE, ANYWHERE]
    if not last:
        shapes.append(jax.ShapeDtypeStruct((2 * LANES, 4 * ROWS), jnp.bfloat16))
        places.append(INSIDE)
    return call(
        functools.partial(project_kernel, quarters, len(columns)),
        tuple(shapes),
        [
            pltpu.VMEM((2, 4 * ROWS, QUARTER), jnp.bfloat16),
            pltpu.VMEM((2, 2 * LANES, QUARTER), jnp.bfloat16),
            pltpu.SemaphoreType.DMA((2, 3)),
            pltpu.SemaphoreType.DMA((2, 2)),
        ],
        limit=LAST,
        in_specs=[INSIDE] * len(columns) + [ANYWHERE] * (1 + len(blocks) + len(last)),
        out_specs=tuple(places),
        input_output_aliases={len(columns) + 1 + len(blocks): 0} if last else {},
    )(*columns, own, *blocks, *last)


def swapped(array):
    return moved(array, lambda y, x, z, c: (y, x, z, 1 - c))


def body(signal, gate, filter_taps, skip_weight, out_weight):
    tables = transform_tables()
    packed, packed_token, mine = call(
        pack_kernel,
        (
            jax.ShapeDtypeStruct((SEQ_DEVICES * 32, LANES), jnp.bfloat16),
            TOKEN,
            jax.ShapeDtypeStruct((ROWS, QUARTER), jnp.bfloat16),
        ),
        [pltpu.VMEM((SEQ_DEVICES * 32, LANES), jnp.float32), pltpu.SemaphoreType.DMA(())],
        work=PACK_WORK,
        in_specs=[INSIDE] * 2 + [ANYWHERE],
        out_specs=(INSIDE, ANYWHERE, ANYWHERE),
    )(signal, filter_taps, out_weight)
    parts = first_quarter(mine)
    blocks = other_quarters(parts, packed_token)
    arrived = lax.all_to_all(
        packed.reshape(SEQ_DEVICES, 32, LANES), AXES, split_axis=0, concat_axis=0, tiled=True
    )
    convolved = call(
        convolve_kernel,
        jax.ShapeDtypeStruct((SEQ_DEVICES * 16, LANES), jnp.bfloat16),
        [
            pltpu.VMEM((SEQ_DEVICES * 32, LANES), jnp.float32),
            pltpu.VMEM((SEQ_DEVICES * 16, LANES), jnp.float32),
        ],
        limit=CONVOLVE,
        work=WORK,
    )(arrived.reshape(SEQ_DEVICES * 32, LANES), *tables)
    returned = lax.all_to_all(
        convolved.reshape(SEQ_DEVICES, 16, LANES), AXES, split_axis=0, concat_axis=0, tiled=True
    )
    channels, shard_len = signal.shape
    mixed, rounded = call(
        mix_kernel,
        (
            jax.ShapeDtypeStruct((channels, shard_len), jnp.float32),
            jax.ShapeDtypeStruct((PIECES, channels, LANES), jnp.bfloat16),
        ),
        [pltpu.VMEM((SEQ_DEVICES * 16, LANES), jnp.float32)],
        limit=MIX,
        work=WORK,
    )(returned.reshape(SEQ_DEVICES * 16, LANES), signal, gate, skip_weight[:, None])
    mine = lax.all_to_all(rounded, "chan", split_axis=0, concat_axis=0, tiled=True)
    mine = mine.reshape(4 * channels, LANES)
    columns = (mine, swapped(mine))
    lower, across, upper = blocks[1], blocks[2:4], blocks[4]
    filled, first, turned = projected_quarters(
        HALVES[0], columns, out_weight, [blocks[0], *across], None
    )
    filled, second = projected_quarters(
        HALVES[1], [turned], out_weight, [lower, upper], filled
    )
    projected = call(
        fill_kernel,
        jax.ShapeDtypeStruct(filled.shape, filled.dtype),
        [pltpu.SemaphoreType.DMA((2, 2))],
        limit=2,
        in_specs=[ANYWHERE] * 3,
        out_specs=ANYWHERE,
        input_output_aliases={0: 0},
    )(filled, swapped(first), swapped(second))
    return mixed, projected


def solution(mesh):
    fine = Mesh(mesh.devices.reshape(4, 4, 2, 2, 4), (*AXES, "chan"))
    slab = P("chan", AXES)
    in_specs = (slab, slab, slab, P("chan"), P("chan", None))
    out_specs = (slab, P((*AXES, "chan"), None))
    return jax.shard_map(body, mesh=fine, in_specs=in_specs, out_specs=out_specs, check_vma=False)
```
